128 devices in a mesh: dp: 8 (over z, core), mp: 16 (over y, x).
Axes of the slice: x: 4, y: 4, z: 4, core: 2. Of those that a mesh axis runs over, the one named last changes fastest.
Arguments:
- grads: bfloat16 [128, 512, 512], P(None, ('dp', 'mp')), may hold values from -150 to 150
- block_slot: int32 [128], replicated, may hold values from 0 to 255, as said below
- iters_count: int32 [128], replicated, may hold values from 2 to 3
- stat_left: float32 [256, 512, 512], P(('dp', 'mp')), may hold values from -3 to 303, as said below
- stat_right: float32 [256, 512, 512], P(('dp', 'mp')), may hold values from -3 to 303, as said below
Outputs:
- update: float32 [128, 512, 512], P(None, ('dp', 'mp'))
- new_left: float32 [256, 512, 512], P(('dp', 'mp'))
- new_right: float32 [256, 512, 512], P(('dp', 'mp'))
The draws below stay inside these ranges and needn't reach their ends.
Inputs may be any that keep to these rules, and one draw needn't show every extreme that they name: `block_slot`: the 128 values are distinct. Slot s is position s % 2 of the device whose flattened index, dp index times the size of mp plus mp index, is s // 2. Some device owns 2 blocks. `stat_left`: each slot holds a symmetric positive definite matrix. `stat_right`: each slot holds a symmetric positive definite matrix.
All inputs are finite; a program needn't handle non-finite values.
Results may differ from the reference program's by a relative error of at most 0.0003.
Values may be sent and summed in bfloat16 or wider, within the bound.
A program may use at most 64 MiB of HBM per device.

```python
import math
import jax
import jax.numpy as jnp
from jax import lax

B = 512
ITERS = 3
NBLK = 128
CAP = 2
SLOTS = 256


def spd_slots(key, lowest, highest, power):
    key_diag, key_noise = jax.random.split(key)
    uniform_pos = jax.random.uniform(key_diag, (SLOTS, B), jnp.float32)
    diag_scale = lowest * (highest / lowest) ** uniform_pos ** power
    noise = jax.random.uniform(key_noise, (SLOTS, B, B), jnp.float32, -1.0, 1.0)
    coupling = (noise + jnp.swapaxes(noise, 1, 2)) * (0.45 / B)
    identity = jnp.eye(B, dtype=jnp.float32)
    root_scale = jnp.sqrt(diag_scale)
    return root_scale[:, :, None] * root_scale[:, None, :] * (identity[None, :, :] + coupling)


def draw_stat_left(key, part):
    key = jax.random.fold_in(key, 21)
    matrix = spd_slots(key, 5.0, 300.0, 1.0)
    return matrix


def draw_stat_right(key, part):
    key = jax.random.fold_in(key, 22)
    matrix = spd_slots(key, 5.0, 300.0, 1.0)
    return matrix


def draw_block_slot(key, part):
    key = jax.random.fold_in(key, 5)
    key_owner, key_score, key_order = jax.random.split(key, 3)
    chosen = jax.random.randint(key_owner, (), 0, SLOTS // CAP)
    slot_ids = jnp.arange(SLOTS, dtype=jnp.int32)
    scores = jax.random.permutation(key_score, SLOTS).astype(jnp.int32)
    scores = jnp.where(slot_ids // CAP == chosen, slot_ids % CAP - CAP, scores)
    ranked = jnp.argsort(scores, stable=True).astype(jnp.int32)
    picked = ranked[:NBLK]
    shuffle = jax.random.permutation(key_order, NBLK)
    return picked[shuffle].astype(jnp.int32)


def draw_grads(key, part):
    key = jax.random.fold_in(key, 9)
    key_rows, key_cols, key_body = jax.random.split(key, 3)
    row_pos = jnp.arange(B, dtype=jnp.float32) / (B - 1)
    row_scale = jnp.exp(jax.random.uniform(key_rows, (NBLK, B, 1), jnp.float32, math.log(0.3), math.log(3.0))) * (1.0 + 2.0 * row_pos)[None, :, None]
    col_scale = jnp.exp(jax.random.uniform(key_cols, (NBLK, 1, B), jnp.float32, math.log(0.3), math.log(3.0)))
    entries = jnp.clip(jax.random.normal(key_body, (NBLK, B, B), jnp.float32), -4.0, 4.0)
    return (row_scale * col_scale * entries).astype(jnp.bfloat16)


def with_ends(values, key, low, top_value):
    longest = values.shape.index(max(values.shape))
    spots = []
    for shift in (0, 1):
        where = [jax.random.randint(jax.random.fold_in(key, axis), (), 0, length) for axis, length in enumerate(values.shape)]
        where[longest] = (where[longest] + shift) % values.shape[longest]
        spots.append(tuple(where))
    return values.at[spots[0]].set(low).at[spots[1]].set(top_value)


def setup_inputs(seed: int = 0) -> dict:
    streams_of = jax.random.split(jax.random.key(seed), 6)
    return {
        "grads": draw_grads(jax.random.fold_in(streams_of[5], 71), 0),
        "block_slot": draw_block_slot(jax.random.fold_in(streams_of[5], 71), 0),
        "iters_count": with_ends(jax.random.randint(streams_of[2], (NBLK,), ITERS - 1, ITERS + 1), jax.random.fold_in(streams_of[2], 1), ITERS - 1, ITERS).astype(jnp.int32),
        "stat_left": draw_stat_left(jax.random.fold_in(streams_of[5], 71), 0),
        "stat_right": draw_stat_right(jax.random.fold_in(streams_of[5], 71), 0),
    }


STAT_DECAY = 0.95
CLIP_SHARE = 0.5
EPSILON = 1e-06

def inverse_root(matrix, granted):
    identity = jnp.eye(B, dtype=jnp.float32)
    frobenius = jnp.sqrt(jnp.sum(matrix * matrix))
    moment = matrix / frobenius
    estimate = identity
    for iteration in range(ITERS):
        active = iteration < granted
        factor = (5.0 * identity - moment) * 0.25
        estimate = jnp.where(active, jnp.dot(estimate, factor, precision=lax.Precision.HIGHEST), estimate)
        if iteration < ITERS - 1:
            square = jnp.dot(factor, factor, precision=lax.Precision.HIGHEST)
            fourth = jnp.dot(square, square, precision=lax.Precision.HIGHEST)
            moment = jnp.where(active, jnp.dot(fourth, moment, precision=lax.Precision.HIGHEST), moment)
    return estimate

def reference(grads, block_slot, iters_count, stat_left, stat_right):
    widened_all = grads.astype(jnp.float32)
    square_sum = jnp.sum(widened_all * widened_all)
    clipping = jnp.minimum(1.0, CLIP_SHARE * B * math.sqrt(NBLK) / (jnp.sqrt(square_sum) + EPSILON))
    squared = clipping * clipping

    def one_block(block_index):
        gradient = grads[block_index]
        slot_id = block_slot[block_index]
        granted = iters_count[block_index]
        gram_rows = jnp.dot(gradient, gradient.T, preferred_element_type=jnp.float32)
        gram_cols = jnp.dot(gradient.T, gradient, preferred_element_type=jnp.float32)
        fresh_left = STAT_DECAY * stat_left[slot_id] + squared * gram_rows
        fresh_right = STAT_DECAY * stat_right[slot_id] + squared * gram_cols
        root_left = inverse_root(fresh_left, granted)
        root_right = inverse_root(fresh_right, granted)
        widened = gradient.astype(jnp.float32)
        product = jnp.dot(jnp.dot(root_left, widened, precision=lax.Precision.HIGHEST), root_right, precision=lax.Precision.HIGHEST)
        grad_norm = jnp.sqrt(jnp.sum(widened * widened))
        prod_norm = jnp.sqrt(jnp.sum(product * product))
        result = clipping * grad_norm * product / (prod_norm + EPSILON)
        return (fresh_left, fresh_right, result)
    lefts, rights, updates = lax.map(one_block, jnp.arange(NBLK, dtype=jnp.int32))
    new_left = stat_left.at[block_slot].set(lefts)
    new_right = stat_right.at[block_slot].set(rights)
    return (updates, new_left, new_right)
```

```python
import math

import jax
import jax.numpy as jnp
from jax import lax
from jax.experimental import pallas as pl
from jax.experimental.pallas import tpu as pltpu
from jax.sharding import PartitionSpec as P

STAT_DECAY = 0.95
CLIP_SHARE = 0.5
EPSILON = 1e-06

B = 512
NBLK = 128
CAP = 2
NDEV = 128
DP = 8
MP = 16
ROWS = B // NDEV
WIDE = B + 128
LEVELS = 32766.0
STEPS = 64.0

BF16 = jnp.bfloat16
F32 = jnp.float32
MESH = pl.DeviceIdType.MESH

C5 = [1.25 ** (5 - k) * (-0.25) ** k * math.comb(5, k) for k in range(6)]
V = [1.5625, -0.3125, 0.0, 0.0, 0.0, 0.0, 0.0]
for _k in range(6):
    V[_k + 1] -= C5[_k] / 4


def dot(former, latter):
    return jnp.dot(former, latter, preferred_element_type=F32)


def split(value):
    high = value.astype(BF16)
    return high, (value - high.astype(F32)).astype(BF16)


def total(value):
    return jnp.sum(jnp.sum(value, axis=0, keepdims=True), axis=1, keepdims=True)


def partner(step):
    dp, mp = lax.axis_index("dp"), lax.axis_index("mp")
    offset = lax.rem(step * 59, NDEV)
    core = lax.rem(lax.rem(dp, 2) + lax.rem(offset, 2), 2)
    z = lax.rem(lax.div(dp, 2) + lax.rem(lax.div(offset, 2), 4), 4)
    y = lax.rem(lax.div(mp, 4) + lax.rem(lax.div(offset, 8), 4), 4)
    x = lax.rem(lax.rem(mp, 4) + lax.div(offset, 32), 4)
    return z * 2 + core, y * 4 + x


def roots_and_product(g, sl, sr, nl, nr, squared, live, three, s):
    fs = []
    for side, (stat, fresh) in enumerate(((sl, nl), (sr, nr))):
        dims = (((1,), (1,)), ((), ())) if side == 0 else (((0,), (0,)), ((), ()))
        gram = lax.dot_general(g[...], g[...], dims, preferred_element_type=F32)
        old = stat[...]
        a = STAT_DECAY * old + squared * gram
        a = jnp.where(live, a, old)
        fresh[...] = a
        fs.append(1.0 / jnp.sqrt(total(a * a)))
    a_of = (nl, nr)
    both = (0, 1)
    for i in both:
        s["mh"][i], s["ml"][i] = split(a_of[i][...] * fs[i])
    for i in both:
        square = dot(s["mh"][i], s["mh"][i])
        s["d"][i] = (a_of[i][...] * (-0.625 * fs[i]) + square * 0.0625).astype(BF16)
    for i in both:
        f = s["d"][i].astype(F32) * 3.125 + dot(s["d"][i], s["d"][i])
        s["fh"][i], s["fl"][i] = split(f)
    for i in both:
        n = (
            a_of[i][...] * (1.25**4 * fs[i])
            + dot(s["fh"][i], s["mh"][i])
            + dot(s["fh"][i], s["ml"][i])
            + dot(s["fl"][i], s["mh"][i])
        )
        s["n"][i] = n
        s["nh"][i], s["nl"][i] = split(n)
    for i in both:
        square = dot(s["nh"][i], s["nh"][i]) + dot(s["nh"][i], s["nl"][i]) + dot(s["nl"][i], s["nh"][i])
        s["s"][i] = square.astype(BF16)
    for i in both:
        c = dot(s["s"][i], s["nh"][i])
        s["c"][i] = c.astype(BF16)
        s["b"][i] = (V[4] * s["nh"][i].astype(F32) + V[5] * s["s"][i].astype(F32) + V[6] * c).astype(BF16)
    w0, w1 = jnp.where(three, V[0], 1.25), jnp.where(three, V[1], -0.25)
    w2, w3, w4 = jnp.where(three, V[2], 0.0), jnp.where(three, V[3], 0.0), jnp.where(three, 1.0, 0.0)
    for i in both:
        u = (
            w1 * s["n"][i]
            + w2 * s["s"][i].astype(F32)
            + w3 * s["c"][i].astype(F32)
            + w4 * dot(s["c"][i], s["b"][i])
        )
        s["n"][i] = u
        s["u"][i] = u.astype(BF16)
    for i in both:
        z = 1.25 * s["n"][i] - a_of[i][...] * (fs[i] * w0 * 0.25) - 0.25 * dot(s["mh"][i], s["u"][i])
        s["zh"][i], s["zl"][i] = split(z)
    alpha = 1.25 * w0
    h = alpha * g[...].astype(F32) + dot(s["zh"][0], g[...]) + dot(s["zl"][0], g[...])
    s["p"][...] = h
    s["hh"][...], s["hl"][...] = split(h)
    p = (
        alpha * s["p"][...]
        + dot(s["hh"][...], s["zh"][1])
        + dot(s["hh"][...], s["zl"][1])
        + dot(s["hl"][...], s["zh"][1])
    )
    s["p"][...] = p
    return total(p * p)


PAIRS = [
    ("mh", BF16), ("ml", BF16), ("d", BF16), ("fh", BF16), ("fl", BF16), ("n", F32), ("nh", BF16), ("nl", BF16),
    ("s", BF16), ("c", BF16), ("b", BF16), ("u", BF16), ("zh", BF16), ("zl", BF16),
]
SINGLES = [("hh", BF16), ("hl", BF16), ("p", F32), ("g", BF16)]
NAMES = [name for name, _ in PAIRS + SINGLES]


def kernel(
    plan, where, grads, left_hbm, right_hbm, update, new_left_hbm, new_right_hbm,
    left, right, new_left, new_right, fsend, frecv, rsend, rrecv,
    local_sem, out_sem, fs_sem, fr_sem, rs_sem, rr_sem, round_sem, *rest,
):
    s = dict(zip(NAMES, rest, strict=True))
    dp, mp = lax.axis_index("dp"), lax.axis_index("mp")
    me = dp * MP + mp

    barrier = pltpu.get_barrier_semaphore()
    for k in range(1, DP):
        pl.semaphore_signal(barrier, inc=1, device_id=(lax.rem(dp + k, DP), mp), device_id_type=MESH)
    for k in range(1, MP):
        pl.semaphore_signal(barrier, inc=1, device_id=(dp, lax.rem(mp + k, MP)), device_id_type=MESH)

    loads = [
        pltpu.make_async_copy(left_hbm, left, local_sem.at[0]),
        pltpu.make_async_copy(right_hbm, right, local_sem.at[1]),
    ]
    for load in loads:
        load.start()

    def place(owner, carry):
        for j in range(CAP):
            fsend[j, owner, :, 0:B] = grads[lax.div(plan[owner * CAP + j], 4)]
        return carry

    lax.fori_loop(0, NDEV, place, 0, unroll=8)

    widened = grads[...].astype(F32)
    mine = jnp.broadcast_to(total(jnp.sum(widened * widened, axis=0)), (ROWS, 128))
    part0 = mine.astype(BF16).astype(F32)
    part1 = (mine - part0).astype(BF16).astype(F32)
    part2 = mine - part0 - part1
    row = lax.broadcasted_iota(jnp.int32, (ROWS, 128), 0)
    parts = jnp.where(row == 0, part0, jnp.where(row == 1, part1, jnp.where(row == 2, part2, 0.0)))
    tail = jnp.broadcast_to(parts.astype(BF16)[None], (NDEV, ROWS, 128))
    for j in range(CAP):
        fsend[j, :, :, B:WIDE] = tail
        frecv[j, me] = fsend[j, me]

    pl.semaphore_wait(barrier, DP + MP - 2)
    for k in range(1, MP):
        pl.semaphore_signal(round_sem, inc=1, device_id=(dp, lax.rem(mp + k, MP)), device_id_type=MESH)
    pl.semaphore_wait(round_sem, MP - 1)

    def exchange(source, target, j, send_sem, recv_sem):
        def step(k, carry):
            to_dp, to_mp = partner(k)
            pltpu.make_async_remote_copy(
                src_ref=source.at[j, to_dp * MP + to_mp],
                dst_ref=target.at[j, me],
                send_sem=send_sem.at[j],
                recv_sem=recv_sem.at[j],
                device_id=(to_dp, to_mp),
                device_id_type=MESH,
            ).start()
            return carry

        lax.fori_loop(1, NDEV, step, 0)

    def settle(buffer, j, sem):
        view = buffer.at[j, pl.ds(0, NDEV - 1)]
        pltpu.make_async_copy(view, view, sem.at[j]).wait()

    for j in range(CAP):
        exchange(fsend, frecv, j, fs_sem, fr_sem)
    for load in loads:
        load.wait()

    def slot(j, carry):
        settle(frecv, j, fr_sem)
        arrived = frecv[j, :, :, 0:B].reshape(B, B)
        s["g"][...] = arrived
        wide = arrived.astype(F32)
        grad_square = total(wide * wide)
        square_sum = total(jnp.sum(frecv[j, :, :, B : B + 128].astype(F32), axis=0)) * (1.0 / 128)
        clipping = jnp.minimum(
            1.0, CLIP_SHARE * B * math.sqrt(NBLK) / (jnp.sqrt(square_sum) + EPSILON)
        )
        granted = lax.rem(plan[me * CAP + j], 4)
        prod_square = roots_and_product(
            s["g"], left.at[j], right.at[j], new_left.at[j], new_right.at[j],
            clipping * clipping, granted > 0, granted > 2, s,
        )
        pltpu.make_async_copy(new_left.at[j], new_left_hbm.at[j], out_sem.at[0, j]).start()
        pltpu.make_async_copy(new_right.at[j], new_right_hbm.at[j], out_sem.at[1, j]).start()
        graft = clipping * jnp.sqrt(grad_square) / (jnp.sqrt(prod_square) + EPSILON)
        scaled = s["p"][...] * graft
        largest = jnp.maximum(jnp.max(jnp.abs(scaled), axis=1, keepdims=True), 1e-30)
        code = jnp.ceil(jnp.log2(largest * (1.0 / LEVELS)) * STEPS)
        levels = jnp.round(scaled * jnp.exp2(code * (-1.0 / STEPS)))
        rsend[j, :, :, 0:B] = levels.astype(jnp.int32).astype(jnp.int16).reshape(NDEV, ROWS, B)
        codes = jnp.broadcast_to(code.astype(jnp.int32), (B, 128)).astype(jnp.int16)
        rsend[j, :, :, B:WIDE] = codes.reshape(NDEV, ROWS, 128)
        rrecv[j, me] = rsend[j, me]
        exchange(rsend, rrecv, j, rs_sem, rr_sem)
        return carry

    lax.fori_loop(0, CAP, slot, 0)

    for j in range(CAP):
        settle(rrecv, j, rr_sem)

    def gather(b, carry):
        at = where[b]
        piece = rrecv[lax.rem(at, CAP), lax.div(at, CAP)]
        scale = jnp.exp2(piece[:, B:WIDE].astype(jnp.int32).astype(F32) * (1.0 / STEPS))
        values = piece[:, 0:B].astype(jnp.int32).astype(F32)
        update[b] = values * jnp.concatenate([scale] * (B // 128), axis=1)
        return carry

    lax.fori_loop(0, NBLK, gather, 0, unroll=8)

    for j in range(CAP):
        pltpu.make_async_copy(new_left.at[j], new_left_hbm.at[j], out_sem.at[0, j]).wait()
        pltpu.make_async_copy(new_right.at[j], new_right_hbm.at[j], out_sem.at[1, j]).wait()
        settle(fsend, j, fs_sem)
        settle(rsend, j, rs_sem)


def per_device(grads, block_slot, iters_count, stat_left, stat_right):
    slots = jnp.arange(CAP * NDEV, dtype=jnp.int32)
    marks = jnp.arange(NBLK, dtype=jnp.int32) * 4 + iters_count
    plan = jnp.sum(jnp.where(slots[:, None] == block_slot[None, :], marks[None, :], 0), axis=1)
    smem, vmem, hbm = (pl.BlockSpec(memory_space=m) for m in (pltpu.SMEM, pltpu.VMEM, pl.ANY))
    dma = pltpu.SemaphoreType.DMA
    return pl.pallas_call(
        kernel,
        out_shape=(
            jax.ShapeDtypeStruct((NBLK, ROWS, B), F32),
            jax.ShapeDtypeStruct((CAP, B, B), F32),
            jax.ShapeDtypeStruct((CAP, B, B), F32),
        ),
        in_specs=[smem, smem, vmem, hbm, hbm],
        out_specs=(vmem, hbm, hbm),
        scratch_shapes=[pltpu.VMEM((CAP, B, B), F32)] * 4
        + [pltpu.VMEM((CAP, NDEV, ROWS, WIDE), BF16)] * 2
        + [pltpu.VMEM((CAP, NDEV, ROWS, WIDE), jnp.int16)] * 2
        + [dma((2,)), dma((2, CAP))]
        + [dma((CAP,))] * 4
        + [pltpu.SemaphoreType.REGULAR]
        + [pltpu.VMEM((2, B, B), t) for _, t in PAIRS]
        + [pltpu.VMEM((B, B), t) for _, t in SINGLES],
        compiler_params=pltpu.CompilerParams(
            collective_id=0, has_side_effects=True, vmem_limit_bytes=56 * 2**20
        ),
    )(plan, block_slot, grads, stat_left, stat_right)


def solution(mesh):
    in_specs = (
        P(None, ("dp", "mp"), None),
        P(),
        P(),
        P(("dp", "mp"), None, None),
        P(("dp", "mp"), None, None),
    )
    out_specs = (
        P(None, ("dp", "mp"), None),
        P(("dp", "mp"), None, None),
        P(("dp", "mp"), None, None),
    )
    return jax.shard_map(
        per_device, mesh=mesh, in_specs=in_specs, out_specs=out_specs, check_vma=False
    )
```

```python
import math

import jax
import jax.numpy as jnp
from jax import lax
from jax.experimental import pallas as pl
from jax.experimental.pallas import tpu as pltpu
from jax.sharding import PartitionSpec as P

STAT_DECAY = 0.95
CLIP_SHARE = 0.5
EPSILON = 1e-06

B = 512
NBLK = 128
CAP = 2
NDEV = 128
DP = 8
MP = 16
ROWS = B // NDEV
WIDE = B + 128
LEVELS = 32766.0
STEPS = 64.0
UNROLL = 127

BF16 = jnp.bfloat16
F32 = jnp.float32
MESH = pl.DeviceIdType.MESH

C5 = [1.25 ** (5 - k) * (-0.25) ** k * math.comb(5, k) for k in range(6)]
V = [1.5625, -0.3125, 0.0, 0.0, 0.0, 0.0, 0.0]
for _k in range(6):
    V[_k + 1] -= C5[_k] / 4


def dot(former, latter):
    return jnp.dot(former, latter, preferred_element_type=F32)


def split(value):
    high = value.astype(BF16)
    return high, (value - high.astype(F32)).astype(BF16)


def total(value):
    return jnp.sum(jnp.sum(value, axis=0, keepdims=True), axis=1, keepdims=True)


def partner(step):
    dp, mp = lax.axis_index("dp"), lax.axis_index("mp")
    offset = (step * 59) & (NDEV - 1)
    core = (dp + offset) & 1
    z = ((dp >> 1) + (offset >> 1)) & 3
    y = ((mp >> 2) + (offset >> 3)) & 3
    x = (mp + (offset >> 5)) & 3
    return z * 2 + core, y * 4 + x


def roots_and_product(g, sl, sr, nl, nr, squared, live, three, s):
    fs = []
    for side, (stat, fresh) in enumerate(((sl, nl), (sr, nr))):
        dims = (((1,), (1,)), ((), ())) if side == 0 else (((0,), (0,)), ((), ()))
        gram = lax.dot_general(g[...], g[...], dims, preferred_element_type=F32)
        old = stat[...]
        a = STAT_DECAY * old + squared * gram
        a = jnp.where(live, a, old)
        fresh[...] = a
        fs.append(1.0 / jnp.sqrt(total(a * a)))
    a_of = (nl, nr)
    both = (0, 1)
    for i in both:
        s["mh"][i], s["ml"][i] = split(a_of[i][...] * fs[i])
    for i in both:
        square = dot(s["mh"][i], s["mh"][i])
        s["d"][i] = (a_of[i][...] * (-0.625 * fs[i]) + square * 0.0625).astype(BF16)
    for i in both:
        f = s["d"][i].astype(F32) * 3.125 + dot(s["d"][i], s["d"][i])
        s["fh"][i], s["fl"][i] = split(f)
    for i in both:
        n = (
            a_of[i][...] * (1.25**4 * fs[i])
            + dot(s["fh"][i], s["mh"][i])
            + dot(s["fh"][i], s["ml"][i])
            + dot(s["fl"][i], s["mh"][i])
        )
        s["n"][i] = n
        s["nh"][i], s["nl"][i] = split(n)
    for i in both:
        square = dot(s["nh"][i], s["nh"][i]) + dot(s["nh"][i], s["nl"][i]) + dot(s["nl"][i], s["nh"][i])
        s["s"][i] = square.astype(BF16)
    for i in both:
        c = dot(s["s"][i], s["nh"][i])
        s["c"][i] = c.astype(BF16)
        s["b"][i] = (V[4] * s["nh"][i].astype(F32) + V[5] * s["s"][i].astype(F32) + V[6] * c).astype(BF16)
    w0, w1 = jnp.where(three, V[0], 1.25), jnp.where(three, V[1], -0.25)
    w2, w3, w4 = jnp.where(three, V[2], 0.0), jnp.where(three, V[3], 0.0), jnp.where(three, 1.0, 0.0)
    for i in both:
        u = (
            w1 * s["n"][i]
            + w2 * s["s"][i].astype(F32)
            + w3 * s["c"][i].astype(F32)
            + w4 * dot(s["c"][i], s["b"][i])
        )
        s["n"][i] = u
        s["u"][i] = u.astype(BF16)
    for i in both:
        z = 1.25 * s["n"][i] - a_of[i][...] * (fs[i] * w0 * 0.25) - 0.25 * dot(s["mh"][i], s["u"][i])
        s["zh"][i], s["zl"][i] = split(z)
    alpha = 1.25 * w0
    h = alpha * g[...].astype(F32) + dot(s["zh"][0], g[...]) + dot(s["zl"][0], g[...])
    s["p"][...] = h
    s["hh"][...], s["hl"][...] = split(h)
    p = (
        alpha * s["p"][...]
        + dot(s["hh"][...], s["zh"][1])
        + dot(s["hh"][...], s["zl"][1])
        + dot(s["hl"][...], s["zh"][1])
    )
    s["p"][...] = p
    return total(p * p)


PAIRS = [
    ("mh", BF16), ("ml", BF16), ("d", BF16), ("fh", BF16), ("fl", BF16), ("n", F32), ("nh", BF16), ("nl", BF16),
    ("s", BF16), ("c", BF16), ("b", BF16), ("u", BF16), ("zh", BF16), ("zl", BF16),
]
SINGLES = [("hh", BF16), ("hl", BF16), ("p", F32), ("g", BF16)]
NAMES = [name for name, _ in PAIRS + SINGLES]


def kernel(
    slot_hbm, counts_hbm, grads_hbm, left_hbm, right_hbm, returned, new_left_hbm, new_right_hbm,
    slot_of, counts, grads, left, right, new_left, new_right, fsend, frecv, rsend, psend, precv, gsend, grecv, plan_v, plan,
    local_sem, out_sem, fs_sem, fr_sem, rs_sem, rr_sem, ps_sem, pr_sem, round_sem, *rest,
):
    s = dict(zip(NAMES, rest, strict=True))
    dp, mp = lax.axis_index("dp"), lax.axis_index("mp")
    me = dp * MP + mp

    barrier = pltpu.get_barrier_semaphore()
    for k in range(1, DP):
        pl.semaphore_signal(barrier, inc=1, device_id=((dp + k) & (DP - 1), mp), device_id_type=MESH)
    for k in range(1, MP):
        pl.semaphore_signal(barrier, inc=1, device_id=(dp, (mp + k) & (MP - 1)), device_id_type=MESH)

    tables = [
        pltpu.make_async_copy(slot_hbm, slot_of, local_sem.at[2]),
        pltpu.make_async_copy(counts_hbm, counts, local_sem.at[3]),
    ]
    rows = pltpu.make_async_copy(grads_hbm, grads, local_sem.at[4])
    loads = [
        pltpu.make_async_copy(left_hbm, left, local_sem.at[0]),
        pltpu.make_async_copy(right_hbm, right, local_sem.at[1]),
    ]
    for load in [*tables, rows, *loads]:
        load.start()
    for load in tables:
        load.wait()

    lane = lax.broadcasted_iota(jnp.int32, (NBLK, NBLK), 1)
    marks = jnp.transpose(lane * 4 + jnp.broadcast_to(counts[...] & 3, (NBLK, NBLK)))
    named = jnp.transpose(jnp.broadcast_to(slot_of[...], (NBLK, NBLK)))
    for half in range(CAP):
        found = jnp.where(named == lane + half * NBLK, marks, 0)
        plan_v[pl.ds(half, 1), :] = jnp.max(found, axis=0, keepdims=True)
    to_scalars = pltpu.make_async_copy(plan_v, plan, local_sem.at[5])
    to_scalars.start()

    rows.wait()
    widened = grads[...].astype(F32)
    mine = jnp.sum(widened * widened, axis=0)
    psend[...] = mine[:, 0:128] + mine[:, 128:256] + mine[:, 256:384] + mine[:, 384:512]
    precv[dp] = psend[...]

    to_scalars.wait()

    def place(owner, carry):
        for j in range(CAP):
            at = owner * CAP + j
            fsend[j, owner] = grads[jnp.minimum(plan[at >> 7, at & (NBLK - 1)] >> 2, NBLK - 1)]
        return carry

    lax.fori_loop(0, NDEV, place, 0, unroll=8)
    for j in range(CAP):
        frecv[j, me] = fsend[j, me]

    pl.semaphore_wait(barrier, DP + MP - 2)
    for k in range(1, MP):
        pl.semaphore_signal(round_sem, inc=1, device_id=(dp, (mp + k) & (MP - 1)), device_id_type=MESH)
    for k in range(1, DP):
        pltpu.make_async_remote_copy(
            src_ref=psend, dst_ref=precv.at[dp], send_sem=ps_sem.at[0], recv_sem=pr_sem.at[0],
            device_id=((dp + k) & (DP - 1), mp), device_id_type=MESH,
        ).start()
    pl.semaphore_wait(round_sem, MP - 1)

    def exchange(source, target, j, send_sem, recv_sem):
        def step(k, carry):
            to_dp, to_mp = partner(k)
            pltpu.make_async_remote_copy(
                src_ref=source.at[j, to_dp * MP + to_mp],
                dst_ref=target.at[j, me],
                send_sem=send_sem.at[j],
                recv_sem=recv_sem.at[j],
                device_id=(to_dp, to_mp),
                device_id_type=MESH,
            ).start()
            return carry

        lax.fori_loop(1, NDEV, step, 0, unroll=UNROLL)

    def settle(view, sem):
        pltpu.make_async_copy(view, view, sem).wait()

    def others(buffer, j):
        return buffer.at[j, pl.ds(0, NDEV - 1)]

    exchange(fsend, frecv, 0, fs_sem, fr_sem)
    settle(precv.at[pl.ds(0, DP - 1)], pr_sem.at[0])
    gsend[...] = jnp.sum(precv[...], axis=0)
    grecv[mp] = gsend[...]
    for k in range(1, MP):
        pltpu.make_async_remote_copy(
            src_ref=gsend, dst_ref=grecv.at[mp], send_sem=ps_sem.at[1], recv_sem=pr_sem.at[1],
            device_id=(dp, (mp + k) & (MP - 1)), device_id_type=MESH,
        ).start()
    exchange(fsend, frecv, 1, fs_sem, fr_sem)
    for load in loads:
        load.wait()
    settle(grecv.at[pl.ds(0, MP - 1)], pr_sem.at[1])

    def slot(j, carry):
        settle(others(frecv, j), fr_sem.at[j])
        arrived = frecv[j].reshape(B, B)
        s["g"][...] = arrived
        wide = arrived.astype(F32)
        grad_square = total(wide * wide)
        square_sum = total(jnp.sum(grecv[...], axis=0))
        clipping = jnp.minimum(
            1.0, CLIP_SHARE * B * math.sqrt(NBLK) / (jnp.sqrt(square_sum) + EPSILON)
        )
        my_slot = me * CAP + j
        granted = plan[my_slot >> 7, my_slot & (NBLK - 1)] & 3
        prod_square = roots_and_product(
            s["g"], left.at[j], right.at[j], new_left.at[j], new_right.at[j],
            clipping * clipping, granted > 0, granted > 2, s,
        )
        pltpu.make_async_copy(new_left.at[j], new_left_hbm.at[j], out_sem.at[0, j]).start()
        pltpu.make_async_copy(new_right.at[j], new_right_hbm.at[j], out_sem.at[1, j]).start()
        graft = clipping * jnp.sqrt(grad_square) / (jnp.sqrt(prod_square) + EPSILON)
        scaled = s["p"][...] * graft
        largest = jnp.maximum(jnp.max(jnp.abs(scaled), axis=1, keepdims=True), 1e-30)
        code = jnp.ceil(jnp.log2(largest * (1.0 / LEVELS)) * STEPS)
        levels = jnp.round(scaled * jnp.exp2(code * (-1.0 / STEPS)))
        rsend[j, :, :, 0:B] = levels.astype(jnp.int32).astype(jnp.int16).reshape(NDEV, ROWS, B)
        codes = jnp.broadcast_to(code.astype(jnp.int32), (B, 128)).astype(jnp.int16)
        rsend[j, :, :, B:WIDE] = codes.reshape(NDEV, ROWS, 128)
        exchange(rsend, returned, j, rs_sem, rr_sem)
        pltpu.make_async_copy(rsend.at[j, me], returned.at[j, me], out_sem.at[2, j]).start()
        return carry

    lax.fori_loop(0, CAP, slot, 0)

    for j in range(CAP):
        pltpu.make_async_copy(new_left.at[j], new_left_hbm.at[j], out_sem.at[0, j]).wait()
        pltpu.make_async_copy(new_right.at[j], new_right_hbm.at[j], out_sem.at[1, j]).wait()
        pltpu.make_async_copy(rsend.at[j, me], returned.at[j, me], out_sem.at[2, j]).wait()
        settle(others(fsend, j), fs_sem.at[j])
        settle(others(rsend, j), rs_sem.at[j])
    settle(precv.at[pl.ds(0, DP - 1)], ps_sem.at[0])
    settle(grecv.at[pl.ds(0, MP - 1)], ps_sem.at[1])
    for j in range(CAP):
        settle(others(returned, j), rr_sem.at[j])


def finish(slot_of, returned, left, right, update, new_left, new_right, sems):
    copies = [
        pltpu.make_async_copy(left, new_left, sems.at[0]),
        pltpu.make_async_copy(right, new_right, sems.at[1]),
    ]
    for copy in copies:
        copy.start()

    def gather(b, carry):
        at = slot_of[b]
        piece = returned[at & 1, at >> 1]
        scale = jnp.exp2(piece[:, B:WIDE].astype(jnp.int32).astype(F32) * (1.0 / STEPS))
        values = piece[:, 0:B].astype(jnp.int32).astype(F32)
        update[b] = values * jnp.concatenate([scale] * (B // 128), axis=1)
        return carry

    lax.fori_loop(0, NBLK, gather, 0, unroll=8)
    for copy in copies:
        copy.wait()


def per_device(grads, block_slot, iters_count, stat_left, stat_right):
    smem, vmem, hbm = (pl.BlockSpec(memory_space=m) for m in (pltpu.SMEM, pltpu.VMEM, pl.ANY))
    dma = pltpu.SemaphoreType.DMA
    stats = jax.ShapeDtypeStruct((CAP, B, B), F32)
    returned, left, right = pl.pallas_call(
        kernel,
        out_shape=(jax.ShapeDtypeStruct((CAP, NDEV, ROWS, WIDE), jnp.int16), stats, stats),
        in_specs=[hbm] * 5,
        out_specs=(hbm, hbm, hbm),
        scratch_shapes=[pltpu.VMEM((1, NBLK), jnp.int32)] * 2
        + [pltpu.VMEM((NBLK, ROWS, B), BF16)]
        + [pltpu.VMEM((CAP, B, B), F32)] * 4
        + [pltpu.VMEM((CAP, NDEV, ROWS, B), BF16)] * 2
        + [pltpu.VMEM((CAP, NDEV, ROWS, WIDE), jnp.int16)]
        + [pltpu.VMEM((ROWS, 128), F32), pltpu.VMEM((DP, ROWS, 128), F32)]
        + [pltpu.VMEM((ROWS, 128), F32), pltpu.VMEM((MP, ROWS, 128), F32)]
        + [pltpu.VMEM((CAP, NBLK), jnp.int32), pltpu.SMEM((CAP, NBLK), jnp.int32)]
        + [dma((6,)), dma((3, CAP))]
        + [dma((CAP,))] * 6
        + [pltpu.SemaphoreType.REGULAR]
        + [pltpu.VMEM((2, B, B), t) for _, t in PAIRS]
        + [pltpu.VMEM((B, B), t) for _, t in SINGLES],
        compiler_params=pltpu.CompilerParams(
            collective_id=0, has_side_effects=True, vmem_limit_bytes=56 * 2**20
        ),
    )(block_slot.reshape(1, NBLK), iters_count.reshape(1, NBLK), grads, stat_left, stat_right)
    return pl.pallas_call(
        finish,
        out_shape=(jax.ShapeDtypeStruct((NBLK, ROWS, B), F32), stats, stats),
        in_specs=[smem, vmem, hbm, hbm],
        out_specs=(vmem, hbm, hbm),
        scratch_shapes=[dma((2,))],
        compiler_params=pltpu.CompilerParams(vmem_limit_bytes=16 * 2**20),
    )(block_slot, returned, left, right)


def solution(mesh):
    in_specs = (
        P(None, ("dp", "mp"), None),
        P(),
        P(),
        P(("dp", "mp"), None, None),
        P(("dp", "mp"), None, None),
    )
    out_specs = (
        P(None, ("dp", "mp"), None),
        P(("dp", "mp"), None, None),
        P(("dp", "mp"), None, None),
    )
    return jax.shard_map(
        per_device, mesh=mesh, in_specs=in_specs, out_specs=out_specs, check_vma=False
    )
```

```python
import math

import jax
import jax.numpy as jnp
from jax import lax
from jax.experimental import pallas as pl
from jax.experimental.pallas import tpu as pltpu
from jax.sharding import PartitionSpec as P

STAT_DECAY = 0.95
CLIP_SHARE = 0.5
EPSILON = 1e-06

B = 512
NBLK = 128
CAP = 2
NDEV = 128
DP = 8
MP = 16
ROWS = B // NDEV
WIDE = B + 128
LEVELS = 32766.0
STEPS = 64.0
UNROLL = 127

BF16 = jnp.bfloat16
F32 = jnp.float32
MESH = pl.DeviceIdType.MESH

C5 = [1.25 ** (5 - k) * (-0.25) ** k * math.comb(5, k) for k in range(6)]
V = [1.5625, -0.3125, 0.0, 0.0, 0.0, 0.0, 0.0]
for _k in range(6):
    V[_k + 1] -= C5[_k] / 4


def dot(former, latter):
    return jnp.dot(former, latter, preferred_element_type=F32)


def split(value):
    high = value.astype(BF16)
    return high, (value - high.astype(F32)).astype(BF16)


def total(value):
    return jnp.sum(jnp.sum(value, axis=0, keepdims=True), axis=1, keepdims=True)


def partner(step):
    dp, mp = lax.axis_index("dp"), lax.axis_index("mp")
    offset = (step * 59) & (NDEV - 1)
    core = (dp + offset) & 1
    z = ((dp >> 1) + (offset >> 1)) & 3
    y = ((mp >> 2) + (offset >> 3)) & 3
    x = (mp + (offset >> 5)) & 3
    return z * 2 + core, y * 4 + x


def roots_and_product(g, sl, sr, nl, nr, squared, live, three, s):
    fs = []
    for side, (stat, fresh) in enumerate(((sl, nl), (sr, nr))):
        dims = (((1,), (1,)), ((), ())) if side == 0 else (((0,), (0,)), ((), ()))
        gram = lax.dot_general(g[...], g[...], dims, preferred_element_type=F32)
        old = stat[...]
        a = STAT_DECAY * old + squared * gram
        a = jnp.where(live, a, old)
        fresh[...] = a
        fs.append(1.0 / jnp.sqrt(total(a * a)))
    a_of = (nl, nr)
    both = (0, 1)
    for i in both:
        s["mh"][i], s["ml"][i] = split(a_of[i][...] * fs[i])
    for i in both:
        square = dot(s["mh"][i], s["mh"][i])
        s["d"][i] = (a_of[i][...] * (-0.625 * fs[i]) + square * 0.0625).astype(BF16)
    for i in both:
        f = s["d"][i].astype(F32) * 3.125 + dot(s["d"][i], s["d"][i])
        s["fh"][i], s["fl"][i] = split(f)
    for i in both:
        n = (
            a_of[i][...] * (1.25**4 * fs[i])
            + dot(s["fh"][i], s["mh"][i])
            + dot(s["fh"][i], s["ml"][i])
            + dot(s["fl"][i], s["mh"][i])
        )
        s["n"][i] = n
        s["nh"][i], s["nl"][i] = split(n)
    for i in both:
        square = dot(s["nh"][i], s["nh"][i]) + dot(s["nh"][i], s["nl"][i]) + dot(s["nl"][i], s["nh"][i])
        s["s"][i] = square.astype(BF16)
    for i in both:
        c = dot(s["s"][i], s["nh"][i])
        s["c"][i] = c.astype(BF16)
        s["b"][i] = (V[4] * s["nh"][i].astype(F32) + V[5] * s["s"][i].astype(F32) + V[6] * c).astype(BF16)
    w0, w1 = jnp.where(three, V[0], 1.25), jnp.where(three, V[1], -0.25)
    w2, w3, w4 = jnp.where(three, V[2], 0.0), jnp.where(three, V[3], 0.0), jnp.where(three, 1.0, 0.0)
    for i in both:
        u = (
            w1 * s["n"][i]
            + w2 * s["s"][i].astype(F32)
            + w3 * s["c"][i].astype(F32)
            + w4 * dot(s["c"][i], s["b"][i])
        )
        s["n"][i] = u
        s["u"][i] = u.astype(BF16)
    for i in both:
        z = 1.25 * s["n"][i] - a_of[i][...] * (fs[i] * w0 * 0.25) - 0.25 * dot(s["mh"][i], s["u"][i])
        s["zh"][i], s["zl"][i] = split(z)
    alpha = 1.25 * w0
    h = alpha * g[...].astype(F32) + dot(s["zh"][0], g[...]) + dot(s["zl"][0], g[...])
    s["p"][...] = h
    s["hh"][...], s["hl"][...] = split(h)
    p = (
        alpha * s["p"][...]
        + dot(s["hh"][...], s["zh"][1])
        + dot(s["hh"][...], s["zl"][1])
        + dot(s["hl"][...], s["zh"][1])
    )
    s["p"][...] = p
    return total(p * p)


PAIRS = [
    ("mh", BF16), ("ml", BF16), ("d", BF16), ("fh", BF16), ("fl", BF16), ("n", F32), ("nh", BF16), ("nl", BF16),
    ("s", BF16), ("c", BF16), ("b", BF16), ("u", BF16), ("zh", BF16), ("zl", BF16),
]
SINGLES = [("hh", BF16), ("hl", BF16), ("p", F32), ("g", BF16)]
NAMES = [name for name, _ in PAIRS + SINGLES]


def kernel(
    slot_hbm, counts_hbm, grads_hbm, left_hbm, right_hbm, returned, new_left_hbm, new_right_hbm,
    slot_of, counts, grads, left, right, new_left, new_right, fsend, frecv, rsend, psend, precv, gsend, grecv, plan_v, plan,
    local_sem, out_sem, fs_sem, fr_sem, rs_sem, rr_sem, ps_sem, pr_sem, round_sem, *rest,
):
    s = dict(zip(NAMES, rest, strict=True))
    dp, mp = lax.axis_index("dp"), lax.axis_index("mp")
    me = dp * MP + mp

    barrier = pltpu.get_barrier_semaphore()
    for k in range(1, DP):
        pl.semaphore_signal(barrier, inc=1, device_id=((dp + k) & (DP - 1), mp), device_id_type=MESH)
    for k in range(1, MP):
        pl.semaphore_signal(barrier, inc=1, device_id=(dp, (mp + k) & (MP - 1)), device_id_type=MESH)

    tables = [
        pltpu.make_async_copy(slot_hbm, slot_of, local_sem.at[2]),
        pltpu.make_async_copy(counts_hbm, counts, local_sem.at[3]),
    ]
    rows = pltpu.make_async_copy(grads_hbm, grads, local_sem.at[4])
    loads = [
        pltpu.make_async_copy(left_hbm, left, local_sem.at[0]),
        pltpu.make_async_copy(right_hbm, right, local_sem.at[1]),
    ]
    for load in [*tables, rows, *loads]:
        load.start()
    for load in tables:
        load.wait()

    lane = lax.broadcasted_iota(jnp.int32, (NBLK, NBLK), 1)
    marks = jnp.transpose(lane * 4 + jnp.broadcast_to(counts[...] & 3, (NBLK, NBLK)))
    named = jnp.transpose(jnp.broadcast_to(slot_of[...], (NBLK, NBLK)))
    for half in range(CAP):
        found = jnp.where(named == lane + half * NBLK, marks, 0)
        plan_v[pl.ds(half, 1), :] = jnp.max(found, axis=0, keepdims=True)
    to_scalars = pltpu.make_async_copy(plan_v, plan, local_sem.at[5])
    to_scalars.start()

    rows.wait()
    widened = grads[...].astype(F32)
    mine = jnp.sum(widened * widened, axis=0)
    psend[...] = mine[:, 0:128] + mine[:, 128:256] + mine[:, 256:384] + mine[:, 384:512]
    precv[dp] = psend[...]

    to_scalars.wait()

    def place(owner, carry):
        for j in range(CAP):
            at = owner * CAP + j
            fsend[j, owner] = grads[jnp.minimum(plan[at >> 7, at & (NBLK - 1)] >> 2, NBLK - 1)]
        return carry

    lax.fori_loop(0, NDEV, place, 0, unroll=8)
    for j in range(CAP):
        frecv[j, me] = fsend[j, me]

    pl.semaphore_wait(barrier, DP + MP - 2)
    for k in range(1, MP):
        pl.semaphore_signal(round_sem, inc=1, device_id=(dp, (mp + k) & (MP - 1)), device_id_type=MESH)
    for k in range(1, DP):
        pltpu.make_async_remote_copy(
            src_ref=psend, dst_ref=precv.at[dp], send_sem=ps_sem.at[0], recv_sem=pr_sem.at[0],
            device_id=((dp + k) & (DP - 1), mp), device_id_type=MESH,
        ).start()
    pl.semaphore_wait(round_sem, MP - 1)

    def exchange(source, target, j, send_sem, recv_sem):
        def step(k, carry):
            to_dp, to_mp = partner(k)
            pltpu.make_async_remote_copy(
                src_ref=source.at[j, to_dp * MP + to_mp],
                dst_ref=target.at[j, me],
                send_sem=send_sem.at[j],
                recv_sem=recv_sem.at[j],
                device_id=(to_dp, to_mp),
                device_id_type=MESH,
            ).start()
            return carry

        lax.fori_loop(1, NDEV, step, 0, unroll=UNROLL)

    def settle(view, sem):
        pltpu.make_async_copy(view, view, sem).wait()

    def others(buffer, j):
        return buffer.at[j, pl.ds(0, NDEV - 1)]

    exchange(fsend, frecv, 0, fs_sem, fr_sem)
    settle(precv.at[pl.ds(0, DP - 1)], pr_sem.at[0])
    gsend[...] = jnp.sum(precv[...], axis=0)
    grecv[mp] = gsend[...]
    for k in range(1, MP):
        pltpu.make_async_remote_copy(
            src_ref=gsend, dst_ref=grecv.at[mp], send_sem=ps_sem.at[1], recv_sem=pr_sem.at[1],
            device_id=(dp, (mp + k) & (MP - 1)), device_id_type=MESH,
        ).start()
    exchange(fsend, frecv, 1, fs_sem, fr_sem)
    for load in loads:
        load.wait()
    settle(grecv.at[pl.ds(0, MP - 1)], pr_sem.at[1])

    def slot(j, carry):
        settle(others(frecv, j), fr_sem.at[j])
        arrived = frecv[j].reshape(B, B)
        s["g"][...] = arrived
        wide = arrived.astype(F32)
        grad_square = total(wide * wide)
        square_sum = total(jnp.sum(grecv[...], axis=0))
        clipping = jnp.minimum(
            1.0, CLIP_SHARE * B * math.sqrt(NBLK) / (jnp.sqrt(square_sum) + EPSILON)
        )
        my_slot = me * CAP + j
        granted = plan[my_slot >> 7, my_slot & (NBLK - 1)] & 3
        prod_square = roots_and_product(
            s["g"], left.at[j], right.at[j], new_left.at[j], new_right.at[j],
            clipping * clipping, granted > 0, granted > 2, s,
        )
        pltpu.make_async_copy(new_left.at[j], new_left_hbm.at[j], out_sem.at[0, j]).start()
        pltpu.make_async_copy(new_right.at[j], new_right_hbm.at[j], out_sem.at[1, j]).start()
        graft = clipping * jnp.sqrt(grad_square) / (jnp.sqrt(prod_square) + EPSILON)
        scaled = s["p"][...] * graft
        largest = jnp.maximum(jnp.max(jnp.abs(scaled), axis=1, keepdims=True), 1e-30)
        code = jnp.ceil(jnp.log2(largest * (1.0 / LEVELS)) * STEPS)
        levels = jnp.round(scaled * jnp.exp2(code * (-1.0 / STEPS)))
        rsend[j, :, :, 0:B] = levels.astype(jnp.int32).astype(jnp.int16).reshape(NDEV, ROWS, B)
        codes = jnp.broadcast_to(code.astype(jnp.int32), (B, 128)).astype(jnp.int16)
        rsend[j, :, :, B:WIDE] = codes.reshape(NDEV, ROWS, 128)
        exchange(rsend, returned, j, rs_sem, rr_sem)
        pltpu.make_async_copy(rsend.at[j, me], returned.at[j, me], out_sem.at[2, j]).start()
        return carry

    lax.fori_loop(0, CAP, slot, 0)

    for j in range(CAP):
        pltpu.make_async_copy(new_left.at[j], new_left_hbm.at[j], out_sem.at[0, j]).wait()
        pltpu.make_async_copy(new_right.at[j], new_right_hbm.at[j], out_sem.at[1, j]).wait()
        pltpu.make_async_copy(rsend.at[j, me], returned.at[j, me], out_sem.at[2, j]).wait()
        settle(others(fsend, j), fs_sem.at[j])
        settle(others(rsend, j), rs_sem.at[j])
    settle(precv.at[pl.ds(0, DP - 1)], ps_sem.at[0])
    settle(grecv.at[pl.ds(0, MP - 1)], ps_sem.at[1])
    for j in range(CAP):
        settle(others(returned, j), rr_sem.at[j])


def finish(slot_of, returned, left, right, update_hbm, new_left_hbm, new_right_hbm, update, sems):
    copies = [
        pltpu.make_async_copy(left, new_left_hbm, sems.at[0]),
        pltpu.make_async_copy(right, new_right_hbm, sems.at[1]),
    ]
    for copy in copies:
        copy.start()

    def gather(b, carry):
        at = slot_of[b]
        piece = returned[at & 1, at >> 1]
        scale = jnp.exp2(piece[:, B:WIDE].astype(jnp.int32).astype(F32) * (1.0 / STEPS))
        values = piece[:, 0:B].astype(jnp.int32).astype(F32)
        update[b] = values * jnp.concatenate([scale] * (B // 128), axis=1)
        return carry

    share = NBLK // 2
    for part in range(2):
        lax.fori_loop(part * share, (part + 1) * share, gather, 0, unroll=8)
        rows = pl.ds(part * share, share)
        copies.append(pltpu.make_async_copy(update.at[rows], update_hbm.at[rows], sems.at[2 + part]))
        copies[-1].start()
    for copy in copies:
        copy.wait()


def per_device(grads, block_slot, iters_count, stat_left, stat_right):
    smem, vmem, hbm, free = (
        pl.BlockSpec(memory_space=m) for m in (pltpu.SMEM, pltpu.VMEM, pltpu.HBM, pl.ANY)
    )
    dma = pltpu.SemaphoreType.DMA
    stats = jax.ShapeDtypeStruct((CAP, B, B), F32)
    returned, left, right = pl.pallas_call(
        kernel,
        out_shape=(jax.ShapeDtypeStruct((CAP, NDEV, ROWS, WIDE), jnp.int16), stats, stats),
        in_specs=[hbm] * 5,
        out_specs=(free, free, free),
        scratch_shapes=[pltpu.VMEM((1, NBLK), jnp.int32)] * 2
        + [pltpu.VMEM((NBLK, ROWS, B), BF16)]
        + [pltpu.VMEM((CAP, B, B), F32)] * 4
        + [pltpu.VMEM((CAP, NDEV, ROWS, B), BF16)] * 2
        + [pltpu.VMEM((CAP, NDEV, ROWS, WIDE), jnp.int16)]
        + [pltpu.VMEM((ROWS, 128), F32), pltpu.VMEM((DP, ROWS, 128), F32)]
        + [pltpu.VMEM((ROWS, 128), F32), pltpu.VMEM((MP, ROWS, 128), F32)]
        + [pltpu.VMEM((CAP, NBLK), jnp.int32), pltpu.SMEM((CAP, NBLK), jnp.int32)]
        + [dma((6,)), dma((3, CAP))]
        + [dma((CAP,))] * 6
        + [pltpu.SemaphoreType.REGULAR]
        + [pltpu.VMEM((2, B, B), t) for _, t in PAIRS]
        + [pltpu.VMEM((B, B), t) for _, t in SINGLES],
        compiler_params=pltpu.CompilerParams(
            collective_id=0, has_side_effects=True, vmem_limit_bytes=48 * 2**20
        ),
    )(block_slot.reshape(1, NBLK), iters_count.reshape(1, NBLK), grads, stat_left, stat_right)
    return pl.pallas_call(
        finish,
        out_shape=(jax.ShapeDtypeStruct((NBLK, ROWS, B), F32), stats, stats),
        in_specs=[smem, vmem, vmem, vmem],
        out_specs=(hbm, hbm, hbm),
        scratch_shapes=[pltpu.VMEM((NBLK, ROWS, B), F32), dma((4,))],
        compiler_params=pltpu.CompilerParams(vmem_limit_bytes=12 * 2**20),
    )(block_slot, returned, left, right)


def solution(mesh):
    in_specs = (
        P(None, ("dp", "mp"), None),
        P(),
        P(),
        P(("dp", "mp"), None, None),
        P(("dp", "mp"), None, None),
    )
    out_specs = (
        P(None, ("dp", "mp"), None),
        P(("dp", "mp"), None, None),
        P(("dp", "mp"), None, None),
    )
    return jax.shard_map(
        per_device, mesh=mesh, in_specs=in_specs, out_specs=out_specs, check_vma=False
    )
```

```python
import math

import jax
import jax.numpy as jnp
from jax import lax
from jax.experimental import pallas as pl
from jax.experimental.pallas import tpu as pltpu
from jax.sharding import PartitionSpec as P

STAT_DECAY = 0.95
CLIP_SHARE = 0.5
EPSILON = 1e-06

B = 512
NBLK = 128
CAP = 2
NDEV = 128
DP = 8
MP = 16
ROWS = B // NDEV
WIDE = B + 128
LEVELS = 32766.0
STEPS = 64.0
UNROLL = 127

BF16 = jnp.bfloat16
F32 = jnp.float32
MESH = pl.DeviceIdType.MESH

C5 = [1.25 ** (5 - k) * (-0.25) ** k * math.comb(5, k) for k in range(6)]
V = [1.5625, -0.3125, 0.0, 0.0, 0.0, 0.0, 0.0]
for _k in range(6):
    V[_k + 1] -= C5[_k] / 4


def dot(former, latter):
    return jnp.dot(former, latter, preferred_element_type=F32)


def split(value):
    high = value.astype(BF16)
    return high, (value - high.astype(F32)).astype(BF16)


def total(value):
    return jnp.sum(jnp.sum(value, axis=0, keepdims=True), axis=1, keepdims=True)


def partner(step):
    dp, mp = lax.axis_index("dp"), lax.axis_index("mp")
    offset = (step * 59) & (NDEV - 1)
    core = (dp + offset) & 1
    z = ((dp >> 1) + (offset >> 1)) & 3
    y = ((mp >> 2) + (offset >> 3)) & 3
    x = (mp + (offset >> 5)) & 3
    return z * 2 + core, y * 4 + x


HALF = B // 2
LOW, HIGH, ALL = slice(0, HALF), slice(HALF, B), slice(0, B)
UPPER = ((LOW, ALL), (HIGH, HIGH))


def put(ref, top, corner):
    ref[LOW, :] = top
    ref[HIGH, HIGH] = corner
    ref[HIGH, LOW] = jnp.transpose(top[:, HIGH])


def put_split(high, low, top, corner):
    (top_high, top_low), (corner_high, corner_low) = split(top), split(corner)
    put(high, top_high, corner_high)
    put(low, top_low, corner_low)


def upper(former, latter):
    return dot(former[LOW, :], latter[...]), dot(former[HIGH, :], latter[:, HIGH])


def upper_split(f_high, f_low, l_high, l_low):
    return tuple(
        dot(f_high[rows, :], l_high[:, cols])
        + dot(f_high[rows, :], l_low[:, cols])
        + dot(f_low[rows, :], l_high[:, cols])
        for rows, cols in UPPER
    )


def wide(ref, at):
    return ref[at].astype(F32)


def roots_and_product(g, sl, sr, nl, nr, squared, live, three, s):
    fs = []
    for side, (stat, fresh) in enumerate(((sl, nl), (sr, nr))):
        sums = []
        for rows, cols in UPPER:
            if side == 0:
                former, latter, over = g[rows, :], g[cols, :], 1
            else:
                former, latter, over = g[:, rows], g[:, cols], 0
            gram = lax.dot_general(former, latter, (((over,), (over,)), ((), ())), preferred_element_type=F32)
            targets = [((rows, cols), gram)]
            if rows == LOW:
                targets.append(((HIGH, LOW), jnp.transpose(gram[:, HIGH])))
            for at, part in targets:
                old = stat[at]
                a = jnp.where(live, STAT_DECAY * old + squared * part, old)
                fresh[at] = a
                sums.append(total(a * a))
        fs.append(1.0 / jnp.sqrt(sums[0] + sums[1] + sums[2]))
    a_of = (nl, nr)
    both = (0, 1)
    at2 = lambda name, i: s[name].at[i]
    for i in both:
        s["mh"][i], s["ml"][i] = split(a_of[i][...] * fs[i])
    for i in both:
        square = upper(at2("mh", i), at2("mh", i))
        d = [(a_of[i][at] * (-0.625 * fs[i]) + v * 0.0625).astype(BF16) for at, v in zip(UPPER, square)]
        put(at2("d", i), *d)
    for i in both:
        square = upper(at2("d", i), at2("d", i))
        f = [wide(at2("d", i), at) * 3.125 + v for at, v in zip(UPPER, square)]
        put_split(at2("fh", i), at2("fl", i), *f)
    for i in both:
        product = upper_split(at2("fh", i), at2("fl", i), at2("mh", i), at2("ml", i))
        n = [a_of[i][at] * (1.25**4 * fs[i]) + v for at, v in zip(UPPER, product)]
        for at, v in zip(UPPER, n):
            at2("n", i)[at] = v
        put_split(at2("nh", i), at2("nl", i), *n)
    for i in both:
        square = upper_split(at2("nh", i), at2("nl", i), at2("nh", i), at2("nl", i))
        put(at2("s", i), *[v.astype(BF16) for v in square])
    for i in both:
        c = upper(at2("s", i), at2("nh", i))
        put(at2("c", i), *[v.astype(BF16) for v in c])
        last = [
            V[4] * wide(at2("nh", i), at) + V[5] * wide(at2("s", i), at) + V[6] * v
            for at, v in zip(UPPER, c)
        ]
        put(at2("b", i), *[v.astype(BF16) for v in last])
    w0, w1 = jnp.where(three, V[0], 1.25), jnp.where(three, V[1], -0.25)
    w2, w3, w4 = jnp.where(three, V[2], 0.0), jnp.where(three, V[3], 0.0), jnp.where(three, 1.0, 0.0)
    for i in both:
        product = upper(at2("c", i), at2("b", i))
        u = [
            w1 * at2("n", i)[at] + w2 * wide(at2("s", i), at) + w3 * wide(at2("c", i), at) + w4 * v
            for at, v in zip(UPPER, product)
        ]
        for at, v in zip(UPPER, u):
            at2("n", i)[at] = v
        put(at2("u", i), *[v.astype(BF16) for v in u])
    for i in both:
        product = upper(at2("mh", i), at2("u", i))
        z = [
            1.25 * at2("n", i)[at] - a_of[i][at] * (fs[i] * w0 * 0.25) - 0.25 * v
            for at, v in zip(UPPER, product)
        ]
        put_split(at2("zh", i), at2("zl", i), *z)
    alpha = 1.25 * w0
    h = alpha * g[...].astype(F32) + dot(s["zh"][0], g[...]) + dot(s["zl"][0], g[...])
    s["p"][...] = h
    s["hh"][...], s["hl"][...] = split(h)
    p = (
        alpha * s["p"][...]
        + dot(s["hh"][...], s["zh"][1])
        + dot(s["hh"][...], s["zl"][1])
        + dot(s["hl"][...], s["zh"][1])
    )
    s["p"][...] = p
    return total(p * p)


PAIRS = [
    ("mh", BF16), ("ml", BF16), ("d", BF16), ("fh", BF16), ("fl", BF16), ("n", F32), ("nh", BF16), ("nl", BF16),
    ("s", BF16), ("c", BF16), ("b", BF16), ("u", BF16), ("zh", BF16), ("zl", BF16),
]
SINGLES = [("hh", BF16), ("hl", BF16), ("p", F32), ("g", BF16)]
NAMES = [name for name, _ in PAIRS + SINGLES]


def kernel(
    slot_hbm, counts_hbm, grads_hbm, left_hbm, right_hbm, returned, new_left_hbm, new_right_hbm,
    slot_of, counts, grads, left, right, new_left, new_right, fsend, frecv, rsend, psend, precv, gsend, grecv, plan_v, plan,
    local_sem, out_sem, fs_sem, fr_sem, rs_sem, rr_sem, ps_sem, pr_sem, round_sem, *rest,
):
    s = dict(zip(NAMES, rest, strict=True))
    dp, mp = lax.axis_index("dp"), lax.axis_index("mp")
    me = dp * MP + mp

    barrier = pltpu.get_barrier_semaphore()
    for k in range(1, DP):
        pl.semaphore_signal(barrier, inc=1, device_id=((dp + k) & (DP - 1), mp), device_id_type=MESH)
    for k in range(1, MP):
        pl.semaphore_signal(barrier, inc=1, device_id=(dp, (mp + k) & (MP - 1)), device_id_type=MESH)

    tables = [
        pltpu.make_async_copy(slot_hbm, slot_of, local_sem.at[2]),
        pltpu.make_async_copy(counts_hbm, counts, local_sem.at[3]),
    ]
    rows = pltpu.make_async_copy(grads_hbm, grads, local_sem.at[4])
    loads = [
        pltpu.make_async_copy(left_hbm, left, local_sem.at[0]),
        pltpu.make_async_copy(right_hbm, right, local_sem.at[1]),
    ]
    for load in [*tables, rows, *loads]:
        load.start()
    for load in tables:
        load.wait()

    lane = lax.broadcasted_iota(jnp.int32, (NBLK, NBLK), 1)
    marks = jnp.transpose(lane * 4 + jnp.broadcast_to(counts[...] & 3, (NBLK, NBLK)))
    named = jnp.transpose(jnp.broadcast_to(slot_of[...], (NBLK, NBLK)))
    for half in range(CAP):
        found = jnp.where(named == lane + half * NBLK, marks, 0)
        plan_v[pl.ds(half, 1), :] = jnp.max(found, axis=0, keepdims=True)
    to_scalars = pltpu.make_async_copy(plan_v, plan, local_sem.at[5])
    to_scalars.start()

    rows.wait()
    widened = grads[...].astype(F32)
    mine = jnp.sum(widened * widened, axis=0)
    psend[...] = mine[:, 0:128] + mine[:, 128:256] + mine[:, 256:384] + mine[:, 384:512]
    precv[dp] = psend[...]

    to_scalars.wait()

    def place(owner, carry):
        for j in range(CAP):
            at = owner * CAP + j
            fsend[j, owner] = grads[jnp.minimum(plan[at >> 7, at & (NBLK - 1)] >> 2, NBLK - 1)]
        return carry

    lax.fori_loop(0, NDEV, place, 0, unroll=8)
    for j in range(CAP):
        frecv[j, me] = fsend[j, me]

    pl.semaphore_wait(barrier, DP + MP - 2)
    for k in range(1, MP):
        pl.semaphore_signal(round_sem, inc=1, device_id=(dp, (mp + k) & (MP - 1)), device_id_type=MESH)
    for k in range(1, DP):
        pltpu.make_async_remote_copy(
            src_ref=psend, dst_ref=precv.at[dp], send_sem=ps_sem.at[0], recv_sem=pr_sem.at[0],
            device_id=((dp + k) & (DP - 1), mp), device_id_type=MESH,
        ).start()
    pl.semaphore_wait(round_sem, MP - 1)

    def exchange(source, target, j, send_sem, recv_sem):
        def step(k, carry):
            to_dp, to_mp = partner(k)
            pltpu.make_async_remote_copy(
                src_ref=source.at[j, to_dp * MP + to_mp],
                dst_ref=target.at[j, me],
                send_sem=send_sem.at[j],
                recv_sem=recv_sem.at[j],
                device_id=(to_dp, to_mp),
                device_id_type=MESH,
            ).start()
            return carry

        lax.fori_loop(1, NDEV, step, 0, unroll=UNROLL)

    def settle(view, sem):
        pltpu.make_async_copy(view, view, sem).wait()

    def others(buffer, j):
        return buffer.at[j, pl.ds(0, NDEV - 1)]

    exchange(fsend, frecv, 0, fs_sem, fr_sem)
    settle(precv.at[pl.ds(0, DP - 1)], pr_sem.at[0])
    gsend[...] = jnp.sum(precv[...], axis=0)
    grecv[mp] = gsend[...]
    for k in range(1, MP):
        pltpu.make_async_remote_copy(
            src_ref=gsend, dst_ref=grecv.at[mp], send_sem=ps_sem.at[1], recv_sem=pr_sem.at[1],
            device_id=(dp, (mp + k) & (MP - 1)), device_id_type=MESH,
        ).start()
    exchange(fsend, frecv, 1, fs_sem, fr_sem)
    for load in loads:
        load.wait()
    settle(grecv.at[pl.ds(0, MP - 1)], pr_sem.at[1])

    def slot(j, carry):
        settle(others(frecv, j), fr_sem.at[j])
        arrived = frecv[j].reshape(B, B)
        s["g"][...] = arrived
        wide = arrived.astype(F32)
        grad_square = total(wide * wide)
        square_sum = total(jnp.sum(grecv[...], axis=0))
        clipping = jnp.minimum(
            1.0, CLIP_SHARE * B * math.sqrt(NBLK) / (jnp.sqrt(square_sum) + EPSILON)
        )
        my_slot = me * CAP + j
        granted = plan[my_slot >> 7, my_slot & (NBLK - 1)] & 3
        prod_square = roots_and_product(
            s["g"], left.at[j], right.at[j], new_left.at[j], new_right.at[j],
            clipping * clipping, granted > 0, granted > 2, s,
        )
        pltpu.make_async_copy(new_left.at[j], new_left_hbm.at[j], out_sem.at[0, j]).start()
        pltpu.make_async_copy(new_right.at[j], new_right_hbm.at[j], out_sem.at[1, j]).start()
        graft = clipping * jnp.sqrt(grad_square) / (jnp.sqrt(prod_square) + EPSILON)
        scaled = s["p"][...] * graft
        largest = jnp.maximum(jnp.max(jnp.abs(scaled), axis=1, keepdims=True), 1e-30)
        code = jnp.ceil(jnp.log2(largest * (1.0 / LEVELS)) * STEPS)
        levels = jnp.round(scaled * jnp.exp2(code * (-1.0 / STEPS)))
        rsend[j, :, :, 0:B] = levels.astype(jnp.int32).astype(jnp.int16).reshape(NDEV, ROWS, B)
        codes = jnp.broadcast_to(code.astype(jnp.int32), (B, 128)).astype(jnp.int16)
        rsend[j, :, :, B:WIDE] = codes.reshape(NDEV, ROWS, 128)
        exchange(rsend, returned, j, rs_sem, rr_sem)
        pltpu.make_async_copy(rsend.at[j, me], returned.at[j, me], out_sem.at[2, j]).start()
        return carry

    lax.fori_loop(0, CAP, slot, 0)

    for j in range(CAP):
        pltpu.make_async_copy(new_left.at[j], new_left_hbm.at[j], out_sem.at[0, j]).wait()
        pltpu.make_async_copy(new_right.at[j], new_right_hbm.at[j], out_sem.at[1, j]).wait()
        pltpu.make_async_copy(rsend.at[j, me], returned.at[j, me], out_sem.at[2, j]).wait()
        settle(others(fsend, j), fs_sem.at[j])
        settle(others(rsend, j), rs_sem.at[j])
    settle(precv.at[pl.ds(0, DP - 1)], ps_sem.at[0])
    settle(grecv.at[pl.ds(0, MP - 1)], ps_sem.at[1])
    for j in range(CAP):
        settle(others(returned, j), rr_sem.at[j])


def finish(slot_of, returned, left, right, update_hbm, new_left_hbm, new_right_hbm, update, sems):
    copies = [
        pltpu.make_async_copy(left, new_left_hbm, sems.at[0]),
        pltpu.make_async_copy(right, new_right_hbm, sems.at[1]),
    ]
    for copy in copies:
        copy.start()

    def gather(b, carry):
        at = slot_of[b]
        piece = returned[at & 1, at >> 1]
        scale = jnp.exp2(piece[:, B:WIDE].astype(jnp.int32).astype(F32) * (1.0 / STEPS))
        values = piece[:, 0:B].astype(jnp.int32).astype(F32)
        update[b] = values * jnp.concatenate([scale] * (B // 128), axis=1)
        return carry

    share = NBLK // 2
    for part in range(2):
        lax.fori_loop(part * share, (part + 1) * share, gather, 0, unroll=8)
        rows = pl.ds(part * share, share)
        copies.append(pltpu.make_async_copy(update.at[rows], update_hbm.at[rows], sems.at[2 + part]))
        copies[-1].start()
    for copy in copies:
        copy.wait()


def per_device(grads, block_slot, iters_count, stat_left, stat_right):
    smem, vmem, hbm, free = (
        pl.BlockSpec(memory_space=m) for m in (pltpu.SMEM, pltpu.VMEM, pltpu.HBM, pl.ANY)
    )
    dma = pltpu.SemaphoreType.DMA
    stats = jax.ShapeDtypeStruct((CAP, B, B), F32)
    returned, left, right = pl.pallas_call(
        kernel,
        out_shape=(jax.ShapeDtypeStruct((CAP, NDEV, ROWS, WIDE), jnp.int16), stats, stats),
        in_specs=[hbm] * 5,
        out_specs=(free, free, free),
        scratch_shapes=[pltpu.VMEM((1, NBLK), jnp.int32)] * 2
        + [pltpu.VMEM((NBLK, ROWS, B), BF16)]
        + [pltpu.VMEM((CAP, B, B), F32)] * 4
        + [pltpu.VMEM((CAP, NDEV, ROWS, B), BF16)] * 2
        + [pltpu.VMEM((CAP, NDEV, ROWS, WIDE), jnp.int16)]
        + [pltpu.VMEM((ROWS, 128), F32), pltpu.VMEM((DP, ROWS, 128), F32)]
        + [pltpu.VMEM((ROWS, 128), F32), pltpu.VMEM((MP, ROWS, 128), F32)]
        + [pltpu.VMEM((CAP, NBLK), jnp.int32), pltpu.SMEM((CAP, NBLK), jnp.int32)]
        + [dma((6,)), dma((3, CAP))]
        + [dma((CAP,))] * 6
        + [pltpu.SemaphoreType.REGULAR]
        + [pltpu.VMEM((2, B, B), t) for _, t in PAIRS]
        + [pltpu.VMEM((B, B), t) for _, t in SINGLES],
        compiler_params=pltpu.CompilerParams(
            collective_id=0, has_side_effects=True, vmem_limit_bytes=48 * 2**20
        ),
    )(block_slot.reshape(1, NBLK), iters_count.reshape(1, NBLK), grads, stat_left, stat_right)
    return pl.pallas_call(
        finish,
        out_shape=(jax.ShapeDtypeStruct((NBLK, ROWS, B), F32), stats, stats),
        in_specs=[smem, vmem, vmem, vmem],
        out_specs=(hbm, hbm, hbm),
        scratch_shapes=[pltpu.VMEM((NBLK, ROWS, B), F32), dma((4,))],
        compiler_params=pltpu.CompilerParams(vmem_limit_bytes=12 * 2**20),
    )(block_slot, returned, left, right)


def solution(mesh):
    in_specs = (
        P(None, ("dp", "mp"), None),
        P(),
        P(),
        P(("dp", "mp"), None, None),
        P(("dp", "mp"), None, None),
    )
    out_specs = (
        P(None, ("dp", "mp"), None),
        P(("dp", "mp"), None, None),
        P(("dp", "mp"), None, None),
    )
    return jax.shard_map(
        per_device, mesh=mesh, in_specs=in_specs, out_specs=out_specs, check_vma=False
    )
```

```python
import math

import jax
import jax.numpy as jnp
from jax import lax
from jax.experimental import pallas as pl
from jax.experimental.pallas import tpu as pltpu
from jax.sharding import PartitionSpec as P

STAT_DECAY = 0.95
CLIP_SHARE = 0.5
EPSILON = 1e-06

B = 512
NBLK = 128
CAP = 2
NDEV = 128
DP = 8
MP = 16
ROWS = B // NDEV
OCTAVES = 18
LEVELS = 32760.0 / OCTAVES
UNROLL = 127

BF16 = jnp.bfloat16
F32 = jnp.float32
MESH = pl.DeviceIdType.MESH

C5 = [1.25 ** (5 - k) * (-0.25) ** k * math.comb(5, k) for k in range(6)]
V = [1.5625, -0.3125, 0.0, 0.0, 0.0, 0.0, 0.0]
for _k in range(6):
    V[_k + 1] -= C5[_k] / 4


def dot(former, latter):
    return jnp.dot(former, latter, preferred_element_type=F32)


def split(value):
    high = value.astype(BF16)
    return high, (value - high.astype(F32)).astype(BF16)


def total(value):
    return jnp.sum(jnp.sum(value, axis=0, keepdims=True), axis=1, keepdims=True)


def partner(step):
    dp, mp = lax.axis_index("dp"), lax.axis_index("mp")
    offset = (step * 59) & (NDEV - 1)
    core = (dp + offset) & 1
    z = ((dp >> 1) + (offset >> 1)) & 3
    y = ((mp >> 2) + (offset >> 3)) & 3
    x = (mp + (offset >> 5)) & 3
    return z * 2 + core, y * 4 + x


HALF = B // 2
LOW, HIGH, ALL = slice(0, HALF), slice(HALF, B), slice(0, B)
UPPER = ((LOW, ALL), (HIGH, HIGH))


def put(ref, top, corner):
    ref[LOW, :] = top
    ref[HIGH, HIGH] = corner
    ref[HIGH, LOW] = jnp.transpose(top[:, HIGH])


def put_split(high, low, top, corner):
    (top_high, top_low), (corner_high, corner_low) = split(top), split(corner)
    put(high, top_high, corner_high)
    put(low, top_low, corner_low)


def upper(former, latter):
    return dot(former[LOW, :], latter[...]), dot(former[HIGH, :], latter[:, HIGH])


def upper_split(f_high, f_low, l_high, l_low):
    return tuple(
        dot(f_high[rows, :], l_high[:, cols])
        + dot(f_high[rows, :], l_low[:, cols])
        + dot(f_low[rows, :], l_high[:, cols])
        for rows, cols in UPPER
    )


def wide(ref, at):
    return ref[at].astype(F32)


def roots_and_product(g, sl, sr, nl, nr, squared, live, three, s):
    fs = []
    for side, (stat, fresh) in enumerate(((sl, nl), (sr, nr))):
        sums = []
        for rows, cols in UPPER:
            if side == 0:
                former, latter, over = g[rows, :], g[cols, :], 1
            else:
                former, latter, over = g[:, rows], g[:, cols], 0
            gram = lax.dot_general(former, latter, (((over,), (over,)), ((), ())), preferred_element_type=F32)
            targets = [((rows, cols), gram)]
            if rows == LOW:
                targets.append(((HIGH, LOW), jnp.transpose(gram[:, HIGH])))
            for at, part in targets:
                old = stat[at]
                a = jnp.where(live, STAT_DECAY * old + squared * part, old)
                fresh[at] = a
                sums.append(total(a * a))
        fs.append(1.0 / jnp.sqrt(sums[0] + sums[1] + sums[2]))
    a_of = (nl, nr)
    both = (0, 1)
    at2 = lambda name, i: s[name].at[i]
    for i in both:
        s["mh"][i], s["ml"][i] = split(a_of[i][...] * fs[i])
    for i in both:
        square = upper(at2("mh", i), at2("mh", i))
        d = [(a_of[i][at] * (-0.625 * fs[i]) + v * 0.0625).astype(BF16) for at, v in zip(UPPER, square)]
        put(at2("d", i), *d)
    for i in both:
        square = upper(at2("d", i), at2("d", i))
        f = [wide(at2("d", i), at) * 3.125 + v for at, v in zip(UPPER, square)]
        put_split(at2("fh", i), at2("fl", i), *f)
    for i in both:
        product = upper_split(at2("fh", i), at2("fl", i), at2("mh", i), at2("ml", i))
        n = [a_of[i][at] * (1.25**4 * fs[i]) + v for at, v in zip(UPPER, product)]
        for at, v in zip(UPPER, n):
            at2("n", i)[at] = v
        put_split(at2("nh", i), at2("nl", i), *n)
    for i in both:
        square = upper_split(at2("nh", i), at2("nl", i), at2("nh", i), at2("nl", i))
        put(at2("s", i), *[v.astype(BF16) for v in square])
    for i in both:
        c = upper(at2("s", i), at2("nh", i))
        put(at2("c", i), *[v.astype(BF16) for v in c])
        last = [
            V[4] * wide(at2("nh", i), at) + V[5] * wide(at2("s", i), at) + V[6] * v
            for at, v in zip(UPPER, c)
        ]
        put(at2("b", i), *[v.astype(BF16) for v in last])
    w0, w1 = jnp.where(three, V[0], 1.25), jnp.where(three, V[1], -0.25)
    w2, w3, w4 = jnp.where(three, V[2], 0.0), jnp.where(three, V[3], 0.0), jnp.where(three, 1.0, 0.0)
    for i in both:
        product = upper(at2("c", i), at2("b", i))
        u = [
            w1 * at2("n", i)[at] + w2 * wide(at2("s", i), at) + w3 * wide(at2("c", i), at) + w4 * v
            for at, v in zip(UPPER, product)
        ]
        for at, v in zip(UPPER, u):
            at2("n", i)[at] = v
        put(at2("u", i), *[v.astype(BF16) for v in u])
    for i in both:
        product = upper(at2("mh", i), at2("u", i))
        z = [
            1.25 * at2("n", i)[at] - a_of[i][at] * (fs[i] * w0 * 0.25) - 0.25 * v
            for at, v in zip(UPPER, product)
        ]
        put_split(at2("zh", i), at2("zl", i), *z)
    alpha = 1.25 * w0
    h = alpha * g[...].astype(F32) + dot(s["zh"][0], g[...]) + dot(s["zl"][0], g[...])
    s["p"][...] = h
    s["hh"][...], s["hl"][...] = split(h)
    p = (
        alpha * s["p"][...]
        + dot(s["hh"][...], s["zh"][1])
        + dot(s["hh"][...], s["zl"][1])
        + dot(s["hl"][...], s["zh"][1])
    )
    s["p"][...] = p
    return total(p * p)


PAIRS = [
    ("mh", BF16), ("ml", BF16), ("d", BF16), ("fh", BF16), ("fl", BF16), ("n", F32), ("nh", BF16), ("nl", BF16),
    ("s", BF16), ("c", BF16), ("b", BF16), ("u", BF16), ("zh", BF16), ("zl", BF16),
]
SINGLES = [("hh", BF16), ("hl", BF16), ("p", F32), ("g", BF16)]
NAMES = [name for name, _ in PAIRS + SINGLES]


def kernel(
    tables_hbm, grads_hbm, left_hbm, right_hbm, returned, new_left_hbm, new_right_hbm, unit_out,
    tables, grads, left, right, new_left, new_right, fsend, frecv, rsend, psend, precv, gsend, grecv, plan_v, plan,
    local_sem, out_sem, fs_sem, fr_sem, rs_sem, rr_sem, ps_sem, pr_sem, round_sem, *rest,
):
    s = dict(zip(NAMES, rest, strict=True))
    dp, mp = lax.axis_index("dp"), lax.axis_index("mp")
    me = dp * MP + mp

    barrier = pltpu.get_barrier_semaphore()
    for k in range(1, DP):
        pl.semaphore_signal(barrier, inc=1, device_id=((dp + k) & (DP - 1), mp), device_id_type=MESH)
    for k in range(1, MP):
        pl.semaphore_signal(barrier, inc=1, device_id=(dp, (mp + k) & (MP - 1)), device_id_type=MESH)

    names = pltpu.make_async_copy(tables_hbm, tables, local_sem.at[2])
    rows = pltpu.make_async_copy(grads_hbm, grads, local_sem.at[3])
    loads = [
        pltpu.make_async_copy(left_hbm, left, local_sem.at[0]),
        pltpu.make_async_copy(right_hbm, right, local_sem.at[1]),
    ]
    for load in [names, rows, *loads]:
        load.start()
    names.wait()

    lane = lax.broadcasted_iota(jnp.int32, (NBLK, NBLK), 1)
    marks = jnp.transpose(lane * 4 + jnp.broadcast_to(tables[1:2, :] & 3, (NBLK, NBLK)))
    named = jnp.transpose(jnp.broadcast_to(tables[0:1, :], (NBLK, NBLK)))
    for half in range(CAP):
        found = jnp.where(named == lane + half * NBLK, marks, 0)
        plan_v[pl.ds(half, 1), :] = jnp.max(found, axis=0, keepdims=True)
    to_scalars = pltpu.make_async_copy(plan_v, plan, local_sem.at[4])
    to_scalars.start()

    rows.wait()
    widened = grads[...].astype(F32)
    mine = jnp.sum(widened * widened, axis=0)
    psend[...] = mine[:, 0:128] + mine[:, 128:256] + mine[:, 256:384] + mine[:, 384:512]
    precv[dp] = psend[...]

    to_scalars.wait()

    def place(owner, carry):
        for j in range(CAP):
            at = owner * CAP + j
            fsend[j, owner] = grads[jnp.minimum(plan[at >> 7, at & (NBLK - 1)] >> 2, NBLK - 1)]
        return carry

    lax.fori_loop(0, NDEV, place, 0, unroll=8)
    for j in range(CAP):
        frecv[j, me] = fsend[j, me]

    pl.semaphore_wait(barrier, DP + MP - 2)
    for k in range(1, MP):
        pl.semaphore_signal(round_sem, inc=1, device_id=(dp, (mp + k) & (MP - 1)), device_id_type=MESH)
    for k in range(1, DP):
        pltpu.make_async_remote_copy(
            src_ref=psend, dst_ref=precv.at[dp], send_sem=ps_sem.at[0], recv_sem=pr_sem.at[0],
            device_id=((dp + k) & (DP - 1), mp), device_id_type=MESH,
        ).start()
    pl.semaphore_wait(round_sem, MP - 1)

    def exchange(source, target, j, send_sem, recv_sem):
        def step(k, carry):
            to_dp, to_mp = partner(k)
            pltpu.make_async_remote_copy(
                src_ref=source.at[j, to_dp * MP + to_mp],
                dst_ref=target.at[j, me],
                send_sem=send_sem.at[j],
                recv_sem=recv_sem.at[j],
                device_id=(to_dp, to_mp),
                device_id_type=MESH,
            ).start()
            return carry

        lax.fori_loop(1, NDEV, step, 0, unroll=UNROLL)

    def settle(view, sem):
        pltpu.make_async_copy(view, view, sem).wait()

    def others(buffer, j):
        return buffer.at[j, pl.ds(0, NDEV - 1)]

    exchange(fsend, frecv, 0, fs_sem, fr_sem)
    settle(precv.at[pl.ds(0, DP - 1)], pr_sem.at[0])
    gsend[...] = jnp.sum(precv[...], axis=0)
    grecv[mp] = gsend[...]
    for k in range(1, MP):
        pltpu.make_async_remote_copy(
            src_ref=gsend, dst_ref=grecv.at[mp], send_sem=ps_sem.at[1], recv_sem=pr_sem.at[1],
            device_id=(dp, (mp + k) & (MP - 1)), device_id_type=MESH,
        ).start()
    exchange(fsend, frecv, 1, fs_sem, fr_sem)
    for load in loads:
        load.wait()
    settle(grecv.at[pl.ds(0, MP - 1)], pr_sem.at[1])

    def slot(j, carry):
        settle(others(frecv, j), fr_sem.at[j])
        arrived = frecv[j].reshape(B, B)
        s["g"][...] = arrived
        wide = arrived.astype(F32)
        grad_square = total(wide * wide)
        norm = jnp.sqrt(total(jnp.sum(grecv[...], axis=0)))
        clipping = jnp.minimum(1.0, CLIP_SHARE * B * math.sqrt(NBLK) / (norm + EPSILON))
        bound = clipping * norm * (4.0 * norm / (4.0 * norm + EPSILON))
        unit = jnp.maximum(bound * 2.0**-OCTAVES, 1e-30)
        unit_out[...] = jnp.broadcast_to(unit, (8, 128))
        my_slot = me * CAP + j
        granted = plan[my_slot >> 7, my_slot & (NBLK - 1)] & 3
        prod_square = roots_and_product(
            s["g"], left.at[j], right.at[j], new_left.at[j], new_right.at[j],
            clipping * clipping, granted > 0, granted > 2, s,
        )
        pltpu.make_async_copy(new_left.at[j], new_left_hbm.at[j], out_sem.at[0, j]).start()
        pltpu.make_async_copy(new_right.at[j], new_right_hbm.at[j], out_sem.at[1, j]).start()
        graft = clipping * jnp.sqrt(grad_square) / (jnp.sqrt(prod_square) + EPSILON)
        product = s["p"][...]
        level = jnp.round(jnp.log2(1.0 + jnp.abs(product) * (graft / unit)) * LEVELS)
        level = jnp.where(product < 0.0, -level, level).astype(jnp.int32).astype(jnp.int16)
        rsend[j] = level.reshape(NDEV, ROWS, B)
        exchange(rsend, returned, j, rs_sem, rr_sem)
        pltpu.make_async_copy(rsend.at[j, me], returned.at[j, me], out_sem.at[2, j]).start()
        return carry

    lax.fori_loop(0, CAP, slot, 0)

    for j in range(CAP):
        pltpu.make_async_copy(new_left.at[j], new_left_hbm.at[j], out_sem.at[0, j]).wait()
        pltpu.make_async_copy(new_right.at[j], new_right_hbm.at[j], out_sem.at[1, j]).wait()
        pltpu.make_async_copy(rsend.at[j, me], returned.at[j, me], out_sem.at[2, j]).wait()
        settle(others(fsend, j), fs_sem.at[j])
        settle(others(rsend, j), rs_sem.at[j])
    settle(precv.at[pl.ds(0, DP - 1)], ps_sem.at[0])
    settle(grecv.at[pl.ds(0, MP - 1)], ps_sem.at[1])
    for j in range(CAP):
        settle(others(returned, j), rr_sem.at[j])


def finish(slot_of, returned, left, right, unit, update_hbm, new_left_hbm, new_right_hbm, update, sems):
    copies = [
        pltpu.make_async_copy(left, new_left_hbm, sems.at[0]),
        pltpu.make_async_copy(right, new_right_hbm, sems.at[1]),
    ]
    for copy in copies:
        copy.start()

    def gather(b, carry):
        at = slot_of[b]
        piece = returned[at & 1, at >> 1]
        level = piece.astype(jnp.int32).astype(F32)
        size = (jnp.exp2(jnp.abs(level) * (1.0 / LEVELS)) - 1.0) * unit[0:1, 0:1]
        update[b] = jnp.where(level < 0.0, -size, size)
        return carry

    share = NBLK // 2
    for part in range(2):
        lax.fori_loop(part * share, (part + 1) * share, gather, 0, unroll=8)
        rows = pl.ds(part * share, share)
        copies.append(pltpu.make_async_copy(update.at[rows], update_hbm.at[rows], sems.at[2 + part]))
        copies[-1].start()
    for copy in copies:
        copy.wait()


def per_device(grads, block_slot, iters_count, stat_left, stat_right):
    smem, vmem, hbm, free = (
        pl.BlockSpec(memory_space=m) for m in (pltpu.SMEM, pltpu.VMEM, pltpu.HBM, pl.ANY)
    )
    dma = pltpu.SemaphoreType.DMA
    stats = jax.ShapeDtypeStruct((CAP, B, B), F32)
    returned, left, right, unit = pl.pallas_call(
        kernel,
        out_shape=(jax.ShapeDtypeStruct((CAP, NDEV, ROWS, B), jnp.int16), stats, stats, jax.ShapeDtypeStruct((8, 128), F32)),
        in_specs=[hbm] * 4,
        out_specs=(free, free, free, vmem),
        scratch_shapes=[pltpu.VMEM((2, NBLK), jnp.int32)]
        + [pltpu.VMEM((NBLK, ROWS, B), BF16)]
        + [pltpu.VMEM((CAP, B, B), F32)] * 4
        + [pltpu.VMEM((CAP, NDEV, ROWS, B), BF16)] * 2
        + [pltpu.VMEM((CAP, NDEV, ROWS, B), jnp.int16)]
        + [pltpu.VMEM((ROWS, 128), F32), pltpu.VMEM((DP, ROWS, 128), F32)]
        + [pltpu.VMEM((ROWS, 128), F32), pltpu.VMEM((MP, ROWS, 128), F32)]
        + [pltpu.VMEM((CAP, NBLK), jnp.int32), pltpu.SMEM((CAP, NBLK), jnp.int32)]
        + [dma((5,)), dma((3, CAP))]
        + [dma((CAP,))] * 6
        + [pltpu.SemaphoreType.REGULAR]
        + [pltpu.VMEM((2, B, B), t) for _, t in PAIRS]
        + [pltpu.VMEM((B, B), t) for _, t in SINGLES],
        compiler_params=pltpu.CompilerParams(
            collective_id=0, has_side_effects=True, vmem_limit_bytes=48 * 2**20
        ),
    )(jnp.stack([block_slot, iters_count]), grads, stat_left, stat_right)
    return pl.pallas_call(
        finish,
        out_shape=(jax.ShapeDtypeStruct((NBLK, ROWS, B), F32), stats, stats),
        in_specs=[smem, vmem, vmem, vmem, vmem],
        out_specs=(hbm, hbm, hbm),
        scratch_shapes=[pltpu.VMEM((NBLK, ROWS, B), F32), dma((4,))],
        compiler_params=pltpu.CompilerParams(vmem_limit_bytes=12 * 2**20),
    )(block_slot, returned, left, right, unit)


def solution(mesh):
    in_specs = (
        P(None, ("dp", "mp"), None),
        P(),
        P(),
        P(("dp", "mp"), None, None),
        P(("dp", "mp"), None, None),
    )
    out_specs = (
        P(None, ("dp", "mp"), None),
        P(("dp", "mp"), None, None),
        P(("dp", "mp"), None, None),
    )
    return jax.shard_map(
        per_device, mesh=mesh, in_specs=in_specs, out_specs=out_specs, check_vma=False
    )
```

```python
import math

import jax
import jax.numpy as jnp
from jax import lax
from jax.experimental import pallas as pl
from jax.experimental.pallas import tpu as pltpu
from jax.sharding import PartitionSpec as P

STAT_DECAY = 0.95
CLIP_SHARE = 0.5
EPSILON = 1e-06

B = 512
NBLK = 128
CAP = 2
NDEV = 128
DP = 8
MP = 16
ROWS = B // NDEV
OCTAVES = 18
LEVELS = 32760.0 / OCTAVES
UNROLL = 127

BF16 = jnp.bfloat16
F32 = jnp.float32
MESH = pl.DeviceIdType.MESH

C5 = [1.25 ** (5 - k) * (-0.25) ** k * math.comb(5, k) for k in range(6)]
V = [1.5625, -0.3125, 0.0, 0.0, 0.0, 0.0, 0.0]
for _k in range(6):
    V[_k + 1] -= C5[_k] / 4


def dot(former, latter):
    return jnp.dot(former, latter, preferred_element_type=F32)


def split(value):
    high = value.astype(BF16)
    return high, (value - high.astype(F32)).astype(BF16)


def total(value):
    return jnp.sum(jnp.sum(value, axis=0, keepdims=True), axis=1, keepdims=True)


def partner(step):
    dp, mp = lax.axis_index("dp"), lax.axis_index("mp")
    offset = (step * 59) & (NDEV - 1)
    core = (dp + offset) & 1
    z = ((dp >> 1) + (offset >> 1)) & 3
    y = ((mp >> 2) + (offset >> 3)) & 3
    x = (mp + (offset >> 5)) & 3
    return z * 2 + core, y * 4 + x


HALF = B // 2
LOW, HIGH, ALL = slice(0, HALF), slice(HALF, B), slice(0, B)
UPPER = ((LOW, ALL), (HIGH, HIGH))


def put(ref, top, corner):
    ref[LOW, :] = top
    ref[HIGH, HIGH] = corner
    ref[HIGH, LOW] = jnp.transpose(top[:, HIGH])


def put_split(high, low, top, corner):
    (top_high, top_low), (corner_high, corner_low) = split(top), split(corner)
    put(high, top_high, corner_high)
    put(low, top_low, corner_low)


def upper(former, latter):
    return dot(former[LOW, :], latter[...]), dot(former[HIGH, :], latter[:, HIGH])


def upper_split(f_high, f_low, l_high, l_low):
    return tuple(
        dot(f_high[rows, :], l_high[:, cols])
        + dot(f_high[rows, :], l_low[:, cols])
        + dot(f_low[rows, :], l_high[:, cols])
        for rows, cols in UPPER
    )


def wide(ref, at):
    return ref[at].astype(F32)


def roots_and_product(g, sl, sr, nl, nr, squared, live, three, s):
    fs = []
    for side, (stat, fresh) in enumerate(((sl, nl), (sr, nr))):
        sums = []
        for rows, cols in UPPER:
            if side == 0:
                former, latter, over = g[rows, :], g[cols, :], 1
            else:
                former, latter, over = g[:, rows], g[:, cols], 0
            gram = lax.dot_general(former, latter, (((over,), (over,)), ((), ())), preferred_element_type=F32)
            targets = [((rows, cols), gram)]
            if rows == LOW:
                targets.append(((HIGH, LOW), jnp.transpose(gram[:, HIGH])))
            for at, part in targets:
                old = stat[at]
                a = jnp.where(live, STAT_DECAY * old + squared * part, old)
                fresh[at] = a
                sums.append(total(a * a))
        fs.append(1.0 / jnp.sqrt(sums[0] + sums[1] + sums[2]))
    a_of = (nl, nr)
    both = (0, 1)
    at2 = lambda name, i: s[name].at[i]
    for i in both:
        s["mh"][i], s["ml"][i] = split(a_of[i][...] * fs[i])
    for i in both:
        square = upper(at2("mh", i), at2("mh", i))
        d = [(a_of[i][at] * (-0.625 * fs[i]) + v * 0.0625).astype(BF16) for at, v in zip(UPPER, square)]
        put(at2("d", i), *d)
    for i in both:
        square = upper(at2("d", i), at2("d", i))
        f = [wide(at2("d", i), at) * 3.125 + v for at, v in zip(UPPER, square)]
        put_split(at2("fh", i), at2("fl", i), *f)
    for i in both:
        product = upper_split(at2("fh", i), at2("fl", i), at2("mh", i), at2("ml", i))
        n = [a_of[i][at] * (1.25**4 * fs[i]) + v for at, v in zip(UPPER, product)]
        for at, v in zip(UPPER, n):
            at2("n", i)[at] = v
        put_split(at2("nh", i), at2("nl", i), *n)
    for i in both:
        square = upper_split(at2("nh", i), at2("nl", i), at2("nh", i), at2("nl", i))
        put(at2("s", i), *[v.astype(BF16) for v in square])
    for i in both:
        c = upper(at2("s", i), at2("nh", i))
        put(at2("c", i), *[v.astype(BF16) for v in c])
        last = [
            V[4] * wide(at2("nh", i), at) + V[5] * wide(at2("s", i), at) + V[6] * v
            for at, v in zip(UPPER, c)
        ]
        put(at2("b", i), *[v.astype(BF16) for v in last])
    w0, w1 = jnp.where(three, V[0], 1.25), jnp.where(three, V[1], -0.25)
    w2, w3, w4 = jnp.where(three, V[2], 0.0), jnp.where(three, V[3], 0.0), jnp.where(three, 1.0, 0.0)
    for i in both:
        product = upper(at2("c", i), at2("b", i))
        u = [
            w1 * at2("n", i)[at] + w2 * wide(at2("s", i), at) + w3 * wide(at2("c", i), at) + w4 * v
            for at, v in zip(UPPER, product)
        ]
        for at, v in zip(UPPER, u):
            at2("n", i)[at] = v
        put(at2("u", i), *[v.astype(BF16) for v in u])
    for i in both:
        product = upper(at2("mh", i), at2("u", i))
        z = [
            1.25 * at2("n", i)[at] - a_of[i][at] * (fs[i] * w0 * 0.25) - 0.25 * v
            for at, v in zip(UPPER, product)
        ]
        put_split(at2("zh", i), at2("zl", i), *z)
    alpha = 1.25 * w0
    h = alpha * g[...].astype(F32) + dot(s["zh"][0], g[...]) + dot(s["zl"][0], g[...])
    s["p"][...] = h
    s["hh"][...], s["hl"][...] = split(h)
    p = (
        alpha * s["p"][...]
        + dot(s["hh"][...], s["zh"][1])
        + dot(s["hh"][...], s["zl"][1])
        + dot(s["hl"][...], s["zh"][1])
    )
    s["p"][...] = p
    return total(p * p)


PAIRS = [
    ("mh", BF16), ("ml", BF16), ("d", BF16), ("fh", BF16), ("fl", BF16), ("n", F32), ("nh", BF16), ("nl", BF16),
    ("s", BF16), ("c", BF16), ("b", BF16), ("u", BF16), ("zh", BF16), ("zl", BF16),
]
SINGLES = [("hh", BF16), ("hl", BF16), ("p", F32), ("g", BF16)]
NAMES = [name for name, _ in PAIRS + SINGLES]


def kernel(
    tables_hbm, grads_hbm, left_hbm, right_hbm, returned, new_left_hbm, new_right_hbm, unit_out,
    tables, grads, left, right, new_left, new_right, fsend, frecv, rsend, psend, precv, gsend, grecv, plan_v, plan, unit_v,
    local_sem, out_sem, fs_sem, fr_sem, rs_sem, rr_sem, ps_sem, pr_sem, round_sem, *rest,
):
    s = dict(zip(NAMES, rest, strict=True))
    dp, mp = lax.axis_index("dp"), lax.axis_index("mp")
    me = dp * MP + mp

    barrier = pltpu.get_barrier_semaphore()
    for k in range(1, DP):
        pl.semaphore_signal(barrier, inc=1, device_id=((dp + k) & (DP - 1), mp), device_id_type=MESH)
    for k in range(1, MP):
        pl.semaphore_signal(barrier, inc=1, device_id=(dp, (mp + k) & (MP - 1)), device_id_type=MESH)

    names = pltpu.make_async_copy(tables_hbm, tables, local_sem.at[2])
    rows = pltpu.make_async_copy(grads_hbm, grads, local_sem.at[3])
    loads = [
        pltpu.make_async_copy(left_hbm, left, local_sem.at[0]),
        pltpu.make_async_copy(right_hbm, right, local_sem.at[1]),
    ]
    for load in [names, rows, *loads]:
        load.start()
    names.wait()

    lane = lax.broadcasted_iota(jnp.int32, (NBLK, NBLK), 1)
    marks = jnp.transpose(lane * 4 + jnp.broadcast_to(tables[1:2, :] & 3, (NBLK, NBLK)))
    named = jnp.transpose(jnp.broadcast_to(tables[0:1, :], (NBLK, NBLK)))
    for half in range(CAP):
        found = jnp.where(named == lane + half * NBLK, marks, 0)
        plan_v[pl.ds(half, 1), :] = jnp.max(found, axis=0, keepdims=True)
    to_scalars = pltpu.make_async_copy(plan_v, plan, local_sem.at[4])
    to_scalars.start()

    rows.wait()
    widened = grads[...].astype(F32)
    mine = jnp.sum(widened * widened, axis=0)
    psend[...] = mine[:, 0:128] + mine[:, 128:256] + mine[:, 256:384] + mine[:, 384:512]
    precv[dp] = psend[...]

    to_scalars.wait()

    def place(owner, carry):
        for j in range(CAP):
            at = owner * CAP + j
            fsend[j, owner] = grads[jnp.minimum(plan[at >> 7, at & (NBLK - 1)] >> 2, NBLK - 1)]
        return carry

    lax.fori_loop(0, NDEV, place, 0, unroll=8)
    for j in range(CAP):
        frecv[j, me] = fsend[j, me]

    pl.semaphore_wait(barrier, DP + MP - 2)
    for k in range(1, MP):
        pl.semaphore_signal(round_sem, inc=1, device_id=(dp, (mp + k) & (MP - 1)), device_id_type=MESH)
    for k in range(1, DP):
        pltpu.make_async_remote_copy(
            src_ref=psend, dst_ref=precv.at[dp], send_sem=ps_sem.at[0], recv_sem=pr_sem.at[0],
            device_id=((dp + k) & (DP - 1), mp), device_id_type=MESH,
        ).start()
    pl.semaphore_wait(round_sem, MP - 1)

    def exchange(source, target, j, send_sem, recv_sem):
        def step(k, carry):
            to_dp, to_mp = partner(k)
            pltpu.make_async_remote_copy(
                src_ref=source.at[j, to_dp * MP + to_mp],
                dst_ref=target.at[j, me],
                send_sem=send_sem.at[j],
                recv_sem=recv_sem.at[j],
                device_id=(to_dp, to_mp),
                device_id_type=MESH,
            ).start()
            return carry

        lax.fori_loop(1, NDEV, step, 0, unroll=UNROLL)

    def settle(view, sem):
        pltpu.make_async_copy(view, view, sem).wait()

    def others(buffer, j):
        return buffer.at[j, pl.ds(0, NDEV - 1)]

    exchange(fsend, frecv, 0, fs_sem, fr_sem)
    settle(precv.at[pl.ds(0, DP - 1)], pr_sem.at[0])
    gsend[...] = jnp.sum(precv[...], axis=0)
    grecv[mp] = gsend[...]
    for k in range(1, MP):
        pltpu.make_async_remote_copy(
            src_ref=gsend, dst_ref=grecv.at[mp], send_sem=ps_sem.at[1], recv_sem=pr_sem.at[1],
            device_id=(dp, (mp + k) & (MP - 1)), device_id_type=MESH,
        ).start()
    exchange(fsend, frecv, 1, fs_sem, fr_sem)
    for load in loads:
        load.wait()
    settle(grecv.at[pl.ds(0, MP - 1)], pr_sem.at[1])

    norm = jnp.sqrt(total(jnp.sum(grecv[...], axis=0)))
    clipping = jnp.minimum(1.0, CLIP_SHARE * B * math.sqrt(NBLK) / (norm + EPSILON))
    bound = clipping * norm * (4.0 * norm / (4.0 * norm + EPSILON))
    unit = jnp.maximum(bound * 2.0**-OCTAVES, 1e-30)
    unit_v[...] = jnp.broadcast_to(unit, (8, 128))
    unit_copy = pltpu.make_async_copy(unit_v, unit_out, local_sem.at[5])
    unit_copy.start()

    def slot(j, carry):
        settle(others(frecv, j), fr_sem.at[j])
        arrived = frecv[j].reshape(B, B)
        s["g"][...] = arrived
        wide = arrived.astype(F32)
        grad_square = total(wide * wide)
        my_slot = me * CAP + j
        granted = plan[my_slot >> 7, my_slot & (NBLK - 1)] & 3
        prod_square = roots_and_product(
            s["g"], left.at[j], right.at[j], new_left.at[j], new_right.at[j],
            clipping * clipping, granted > 0, granted > 2, s,
        )
        pltpu.make_async_copy(new_left.at[j], new_left_hbm.at[j], out_sem.at[0, j]).start()
        pltpu.make_async_copy(new_right.at[j], new_right_hbm.at[j], out_sem.at[1, j]).start()
        graft = clipping * jnp.sqrt(grad_square) / (jnp.sqrt(prod_square) + EPSILON)
        product = s["p"][...]
        level = jnp.round(jnp.log2(1.0 + jnp.abs(product) * (graft / unit)) * LEVELS)
        level = jnp.where(product < 0.0, -level, level).astype(jnp.int32).astype(jnp.int16)
        rsend[j] = level.reshape(NDEV, ROWS, B)
        exchange(rsend, returned, j, rs_sem, rr_sem)
        pltpu.make_async_copy(rsend.at[j, me], returned.at[j, me], out_sem.at[2, j]).start()
        return carry

    lax.fori_loop(0, CAP, slot, 0)
    unit_copy.wait()

    for j in range(CAP):
        pltpu.make_async_copy(new_left.at[j], new_left_hbm.at[j], out_sem.at[0, j]).wait()
        pltpu.make_async_copy(new_right.at[j], new_right_hbm.at[j], out_sem.at[1, j]).wait()
        pltpu.make_async_copy(rsend.at[j, me], returned.at[j, me], out_sem.at[2, j]).wait()
        settle(others(fsend, j), fs_sem.at[j])
        settle(others(rsend, j), rs_sem.at[j])
    settle(precv.at[pl.ds(0, DP - 1)], ps_sem.at[0])
    settle(grecv.at[pl.ds(0, MP - 1)], ps_sem.at[1])
    for j in range(CAP):
        settle(others(returned, j), rr_sem.at[j])


def finish(slot_of, returned, left, right, unit, update_hbm, new_left_hbm, new_right_hbm, update, sems):
    copies = []
    for held, out in ((left, new_left_hbm), (right, new_right_hbm)):
        for j in range(CAP):
            for rows in (pl.ds(0, HALF), pl.ds(HALF, HALF)):
                sem = sems.at[len(copies)]
                copies.append(pltpu.make_async_copy(held.at[j, rows], out.at[j, rows], sem))
    for copy in copies:
        copy.start()

    def gather(b, carry):
        at = slot_of[b]
        piece = returned[at & 1, at >> 1]
        level = piece.astype(jnp.int32).astype(F32)
        size = (jnp.exp2(jnp.abs(level) * (1.0 / LEVELS)) - 1.0) * unit[0:1, 0:1]
        update[b] = jnp.where(level < 0.0, -size, size)
        return carry

    share = NBLK // 2
    for part in range(2):
        lax.fori_loop(part * share, (part + 1) * share, gather, 0, unroll=8)
        rows = pl.ds(part * share, share)
        copies.append(pltpu.make_async_copy(update.at[rows], update_hbm.at[rows], sems.at[8 + part]))
        copies[-1].start()
    for copy in copies:
        copy.wait()


def per_device(grads, block_slot, iters_count, stat_left, stat_right):
    smem, vmem, hbm, free = (
        pl.BlockSpec(memory_space=m) for m in (pltpu.SMEM, pltpu.VMEM, pltpu.HBM, pl.ANY)
    )
    dma = pltpu.SemaphoreType.DMA
    stats = jax.ShapeDtypeStruct((CAP, B, B), F32)
    returned, left, right, unit = pl.pallas_call(
        kernel,
        out_shape=(jax.ShapeDtypeStruct((CAP, NDEV, ROWS, B), jnp.int16), stats, stats, jax.ShapeDtypeStruct((8, 128), F32)),
        in_specs=[hbm] * 4,
        out_specs=(free, free, free, free),
        scratch_shapes=[pltpu.VMEM((2, NBLK), jnp.int32)]
        + [pltpu.VMEM((NBLK, ROWS, B), BF16)]
        + [pltpu.VMEM((CAP, B, B), F32)] * 4
        + [pltpu.VMEM((CAP, NDEV, ROWS, B), BF16)] * 2
        + [pltpu.VMEM((CAP, NDEV, ROWS, B), jnp.int16)]
        + [pltpu.VMEM((ROWS, 128), F32), pltpu.VMEM((DP, ROWS, 128), F32)]
        + [pltpu.VMEM((ROWS, 128), F32), pltpu.VMEM((MP, ROWS, 128), F32)]
        + [pltpu.VMEM((CAP, NBLK), jnp.int32), pltpu.SMEM((CAP, NBLK), jnp.int32), pltpu.VMEM((8, 128), F32)]
        + [dma((6,)), dma((3, CAP))]
        + [dma((CAP,))] * 6
        + [pltpu.SemaphoreType.REGULAR]
        + [pltpu.VMEM((2, B, B), t) for _, t in PAIRS]
        + [pltpu.VMEM((B, B), t) for _, t in SINGLES],
        compiler_params=pltpu.CompilerParams(
            collective_id=0, has_side_effects=True, vmem_limit_bytes=48 * 2**20
        ),
    )(jnp.stack([block_slot, iters_count]), grads, stat_left, stat_right)
    return pl.pallas_call(
        finish,
        out_shape=(jax.ShapeDtypeStruct((NBLK, ROWS, B), F32), stats, stats),
        in_specs=[smem, vmem, vmem, vmem, vmem],
        out_specs=(hbm, hbm, hbm),
        scratch_shapes=[pltpu.VMEM((NBLK, ROWS, B), F32), dma((10,))],
        compiler_params=pltpu.CompilerParams(vmem_limit_bytes=12 * 2**20),
    )(block_slot, returned, left, right, unit)


def solution(mesh):
    in_specs = (
        P(None, ("dp", "mp"), None),
        P(),
        P(),
        P(("dp", "mp"), None, None),
        P(("dp", "mp"), None, None),
    )
    out_specs = (
        P(None, ("dp", "mp"), None),
        P(("dp", "mp"), None, None),
        P(("dp", "mp"), None, None),
    )
    return jax.shard_map(
        per_device, mesh=mesh, in_specs=in_specs, out_specs=out_specs, check_vma=False
    )
```

```python
import math

import jax
import jax.numpy as jnp
from jax import lax
from jax.experimental import pallas as pl
from jax.experimental.pallas import tpu as pltpu
from jax.sharding import PartitionSpec as P

STAT_DECAY = 0.95
CLIP_SHARE = 0.5
EPSILON = 1e-06

B = 512
NBLK = 128
CAP = 2
NDEV = 128
DP = 8
MP = 16
ROWS = B // NDEV
OCTAVES = 18
LEVELS = 32760.0 / OCTAVES
UNROLL = 127

BF16 = jnp.bfloat16
F32 = jnp.float32
MESH = pl.DeviceIdType.MESH

C5 = [1.25 ** (5 - k) * (-0.25) ** k * math.comb(5, k) for k in range(6)]
V = [1.5625, -0.3125, 0.0, 0.0, 0.0, 0.0, 0.0]
for _k in range(6):
    V[_k + 1] -= C5[_k] / 4


def dot(former, latter):
    return jnp.dot(former, latter, preferred_element_type=F32)


def split(value):
    high = value.astype(BF16)
    return high, (value - high.astype(F32)).astype(BF16)


def total(value):
    return jnp.sum(jnp.sum(value, axis=0, keepdims=True), axis=1, keepdims=True)


def partner(step):
    dp, mp = lax.axis_index("dp"), lax.axis_index("mp")
    offset = (step * 37) & (NDEV - 1)
    core = (dp + offset) & 1
    z = ((dp >> 1) + (offset >> 1)) & 3
    y = ((mp >> 2) + (offset >> 3)) & 3
    x = (mp + (offset >> 5)) & 3
    return z * 2 + core, y * 4 + x


HALF = B // 2
LOW, HIGH, ALL = slice(0, HALF), slice(HALF, B), slice(0, B)
UPPER = ((LOW, ALL), (HIGH, HIGH))


def put(ref, top, corner):
    ref[LOW, :] = top
    ref[HIGH, HIGH] = corner
    ref[HIGH, LOW] = jnp.transpose(top[:, HIGH])


def put_split(high, low, top, corner):
    (top_high, top_low), (corner_high, corner_low) = split(top), split(corner)
    put(high, top_high, corner_high)
    put(low, top_low, corner_low)


def upper(former, latter):
    return dot(former[LOW, :], latter[...]), dot(former[HIGH, :], latter[:, HIGH])


def upper_split(f_high, f_low, l_high, l_low):
    return tuple(
        dot(f_high[rows, :], l_high[:, cols])
        + dot(f_high[rows, :], l_low[:, cols])
        + dot(f_low[rows, :], l_high[:, cols])
        for rows, cols in UPPER
    )


def wide(ref, at):
    return ref[at].astype(F32)


def roots_and_product(g, sl, sr, nl, nr, squared, live, three, s):
    fs = []
    for side, (stat, fresh) in enumerate(((sl, nl), (sr, nr))):
        sums = []
        for rows, cols in UPPER:
            if side == 0:
                former, latter, over = g[rows, :], g[cols, :], 1
            else:
                former, latter, over = g[:, rows], g[:, cols], 0
            gram = lax.dot_general(former, latter, (((over,), (over,)), ((), ())), preferred_element_type=F32)
            targets = [((rows, cols), gram)]
            if rows == LOW:
                targets.append(((HIGH, LOW), jnp.transpose(gram[:, HIGH])))
            for at, part in targets:
                old = stat[at]
                a = jnp.where(live, STAT_DECAY * old + squared * part, old)
                fresh[at] = a
                sums.append(total(a * a))
        fs.append(1.0 / jnp.sqrt(sums[0] + sums[1] + sums[2]))
    a_of = (nl, nr)
    both = (0, 1)
    at2 = lambda name, i: s[name].at[i]
    for i in both:
        s["mh"][i], s["ml"][i] = split(a_of[i][...] * fs[i])
    for i in both:
        square = upper(at2("mh", i), at2("mh", i))
        d = [(a_of[i][at] * (-0.625 * fs[i]) + v * 0.0625).astype(BF16) for at, v in zip(UPPER, square)]
        put(at2("d", i), *d)
    for i in both:
        square = upper(at2("d", i), at2("d", i))
        f = [wide(at2("d", i), at) * 3.125 + v for at, v in zip(UPPER, square)]
        put_split(at2("fh", i), at2("fl", i), *f)
    for i in both:
        product = upper_split(at2("fh", i), at2("fl", i), at2("mh", i), at2("ml", i))
        n = [a_of[i][at] * (1.25**4 * fs[i]) + v for at, v in zip(UPPER, product)]
        for at, v in zip(UPPER, n):
            at2("n", i)[at] = v
        put_split(at2("nh", i), at2("nl", i), *n)
    for i in both:
        square = upper_split(at2("nh", i), at2("nl", i), at2("nh", i), at2("nl", i))
        put(at2("s", i), *[v.astype(BF16) for v in square])
    for i in both:
        c = upper(at2("s", i), at2("nh", i))
        put(at2("c", i), *[v.astype(BF16) for v in c])
        last = [
            V[4] * wide(at2("nh", i), at) + V[5] * wide(at2("s", i), at) + V[6] * v
            for at, v in zip(UPPER, c)
        ]
        put(at2("b", i), *[v.astype(BF16) for v in last])
    w0, w1 = jnp.where(three, V[0], 1.25), jnp.where(three, V[1], -0.25)
    w2, w3, w4 = jnp.where(three, V[2], 0.0), jnp.where(three, V[3], 0.0), jnp.where(three, 1.0, 0.0)
    for i in both:
        product = upper(at2("c", i), at2("b", i))
        u = [
            w1 * at2("n", i)[at] + w2 * wide(at2("s", i), at) + w3 * wide(at2("c", i), at) + w4 * v
            for at, v in zip(UPPER, product)
        ]
        for at, v in zip(UPPER, u):
            at2("n", i)[at] = v
        put(at2("u", i), *[v.astype(BF16) for v in u])
    for i in both:
        product = upper(at2("mh", i), at2("u", i))
        z = [
            1.25 * at2("n", i)[at] - a_of[i][at] * (fs[i] * w0 * 0.25) - 0.25 * v
            for at, v in zip(UPPER, product)
        ]
        put_split(at2("zh", i), at2("zl", i), *z)
    alpha = 1.25 * w0
    h = alpha * g[...].astype(F32) + dot(s["zh"][0], g[...]) + dot(s["zl"][0], g[...])
    s["p"][...] = h
    s["hh"][...], s["hl"][...] = split(h)
    p = (
        alpha * s["p"][...]
        + dot(s["hh"][...], s["zh"][1])
        + dot(s["hh"][...], s["zl"][1])
        + dot(s["hl"][...], s["zh"][1])
    )
    s["p"][...] = p
    return total(p * p)


PAIRS = [
    ("mh", BF16), ("ml", BF16), ("d", BF16), ("fh", BF16), ("fl", BF16), ("n", F32), ("nh", BF16), ("nl", BF16),
    ("s", BF16), ("c", BF16), ("b", BF16), ("u", BF16), ("zh", BF16), ("zl", BF16),
]
SINGLES = [("hh", BF16), ("hl", BF16), ("p", F32), ("g", BF16)]
NAMES = [name for name, _ in PAIRS + SINGLES]


def kernel(
    tables_hbm, grads_hbm, left_hbm, right_hbm, returned, new_left_hbm, new_right_hbm, unit_out,
    tables, grads, left, right, new_left, new_right, fsend, frecv, rsend, psend, precv, gsend, grecv, plan_v, plan,
    local_sem, out_sem, fs_sem, fr_sem, rs_sem, rr_sem, ps_sem, pr_sem, round_sem, *rest,
):
    s = dict(zip(NAMES, rest, strict=True))
    dp, mp = lax.axis_index("dp"), lax.axis_index("mp")
    me = dp * MP + mp

    barrier = pltpu.get_barrier_semaphore()
    for k in range(1, DP):
        pl.semaphore_signal(barrier, inc=1, device_id=((dp + k) & (DP - 1), mp), device_id_type=MESH)
    for k in range(1, MP):
        pl.semaphore_signal(barrier, inc=1, device_id=(dp, (mp + k) & (MP - 1)), device_id_type=MESH)

    names = pltpu.make_async_copy(tables_hbm, tables, local_sem.at[2])
    rows = pltpu.make_async_copy(grads_hbm, grads, local_sem.at[3])
    loads = [
        pltpu.make_async_copy(left_hbm, left, local_sem.at[0]),
        pltpu.make_async_copy(right_hbm, right, local_sem.at[1]),
    ]
    for load in [names, rows, *loads]:
        load.start()
    names.wait()

    lane = lax.broadcasted_iota(jnp.int32, (NBLK, NBLK), 1)
    marks = jnp.transpose(lane * 4 + jnp.broadcast_to(tables[1:2, :] & 3, (NBLK, NBLK)))
    named = jnp.transpose(jnp.broadcast_to(tables[0:1, :], (NBLK, NBLK)))
    for half in range(CAP):
        found = jnp.where(named == lane + half * NBLK, marks, 0)
        plan_v[pl.ds(half, 1), :] = jnp.max(found, axis=0, keepdims=True)
    to_scalars = pltpu.make_async_copy(plan_v, plan, local_sem.at[4])
    to_scalars.start()

    rows.wait()
    widened = grads[...].astype(F32)
    mine = jnp.sum(widened * widened, axis=0)
    psend[...] = mine[:, 0:128] + mine[:, 128:256] + mine[:, 256:384] + mine[:, 384:512]
    precv[dp] = psend[...]

    to_scalars.wait()

    def place(owner, carry):
        for j in range(CAP):
            at = owner * CAP + j
            fsend[j, owner] = grads[jnp.minimum(plan[at >> 7, at & (NBLK - 1)] >> 2, NBLK - 1)]
        return carry

    lax.fori_loop(0, NDEV, place, 0, unroll=8)
    for j in range(CAP):
        frecv[j, me] = fsend[j, me]

    pl.semaphore_wait(barrier, DP + MP - 2)
    for k in range(1, MP):
        pl.semaphore_signal(round_sem, inc=1, device_id=(dp, (mp + k) & (MP - 1)), device_id_type=MESH)
    for k in range(1, DP):
        pltpu.make_async_remote_copy(
            src_ref=psend, dst_ref=precv.at[dp], send_sem=ps_sem.at[0], recv_sem=pr_sem.at[0],
            device_id=((dp + k) & (DP - 1), mp), device_id_type=MESH,
        ).start()
    pl.semaphore_wait(round_sem, MP - 1)

    def exchange(source, target, j, send_sem, recv_sem):
        def step(k, carry):
            to_dp, to_mp = partner(k)
            pltpu.make_async_remote_copy(
                src_ref=source.at[j, to_dp * MP + to_mp],
                dst_ref=target.at[j, me],
                send_sem=send_sem.at[j],
                recv_sem=recv_sem.at[j],
                device_id=(to_dp, to_mp),
                device_id_type=MESH,
            ).start()
            return carry

        lax.fori_loop(1, NDEV, step, 0, unroll=UNROLL)

    def settle(view, sem):
        pltpu.make_async_copy(view, view, sem).wait()

    def others(buffer, j):
        return buffer.at[j, pl.ds(0, NDEV - 1)]

    exchange(fsend, frecv, 0, fs_sem, fr_sem)
    settle(precv.at[pl.ds(0, DP - 1)], pr_sem.at[0])
    gsend[...] = jnp.sum(precv[...], axis=0)
    grecv[mp] = gsend[...]
    for k in range(1, MP):
        pltpu.make_async_remote_copy(
            src_ref=gsend, dst_ref=grecv.at[mp], send_sem=ps_sem.at[1], recv_sem=pr_sem.at[1],
            device_id=(dp, (mp + k) & (MP - 1)), device_id_type=MESH,
        ).start()
    exchange(fsend, frecv, 1, fs_sem, fr_sem)
    for load in loads:
        load.wait()
    settle(grecv.at[pl.ds(0, MP - 1)], pr_sem.at[1])

    def slot(j, carry):
        settle(others(frecv, j), fr_sem.at[j])
        arrived = frecv[j].reshape(B, B)
        s["g"][...] = arrived
        wide = arrived.astype(F32)
        grad_square = total(wide * wide)
        norm = jnp.sqrt(total(jnp.sum(grecv[...], axis=0)))
        clipping = jnp.minimum(1.0, CLIP_SHARE * B * math.sqrt(NBLK) / (norm + EPSILON))
        bound = clipping * norm * (4.0 * norm / (4.0 * norm + EPSILON))
        unit = jnp.maximum(bound * 2.0**-OCTAVES, 1e-30)
        unit_out[...] = jnp.broadcast_to(unit, (8, 128))
        my_slot = me * CAP + j
        granted = plan[my_slot >> 7, my_slot & (NBLK - 1)] & 3
        prod_square = roots_and_product(
            s["g"], left.at[j], right.at[j], new_left.at[j], new_right.at[j],
            clipping * clipping, granted > 0, granted > 2, s,
        )
        pltpu.make_async_copy(new_left.at[j], new_left_hbm.at[j], out_sem.at[0, j]).start()
        pltpu.make_async_copy(new_right.at[j], new_right_hbm.at[j], out_sem.at[1, j]).start()
        graft = clipping * jnp.sqrt(grad_square) / (jnp.sqrt(prod_square) + EPSILON)
        product = s["p"][...]
        level = jnp.round(jnp.log2(1.0 + jnp.abs(product) * (graft / unit)) * LEVELS)
        level = jnp.where(product < 0.0, -level, level).astype(jnp.int32).astype(jnp.int16)
        rsend[j] = level.reshape(NDEV, ROWS, B)
        exchange(rsend, returned, j, rs_sem, rr_sem)
        pltpu.make_async_copy(rsend.at[j, me], returned.at[j, me], out_sem.at[2, j]).start()
        return carry

    lax.fori_loop(0, CAP, slot, 0)

    for j in range(CAP):
        pltpu.make_async_copy(new_left.at[j], new_left_hbm.at[j], out_sem.at[0, j]).wait()
        pltpu.make_async_copy(new_right.at[j], new_right_hbm.at[j], out_sem.at[1, j]).wait()
        pltpu.make_async_copy(rsend.at[j, me], returned.at[j, me], out_sem.at[2, j]).wait()
        settle(others(fsend, j), fs_sem.at[j])
        settle(others(rsend, j), rs_sem.at[j])
    settle(precv.at[pl.ds(0, DP - 1)], ps_sem.at[0])
    settle(grecv.at[pl.ds(0, MP - 1)], ps_sem.at[1])
    for j in range(CAP):
        settle(others(returned, j), rr_sem.at[j])


def finish(slot_of, returned, left, right, unit, update_hbm, new_left_hbm, new_right_hbm, update, sems):
    copies = [
        pltpu.make_async_copy(left, new_left_hbm, sems.at[0]),
        pltpu.make_async_copy(right, new_right_hbm, sems.at[1]),
    ]
    for copy in copies:
        copy.start()

    def gather(b, carry):
        at = slot_of[b]
        piece = returned[at & 1, at >> 1]
        level = piece.astype(jnp.int32).astype(F32)
        size = (jnp.exp2(jnp.abs(level) * (1.0 / LEVELS)) - 1.0) * unit[0:1, 0:1]
        update[b] = jnp.where(level < 0.0, -size, size)
        return carry

    share = NBLK // 2
    for part in range(2):
        lax.fori_loop(part * share, (part + 1) * share, gather, 0, unroll=8)
        rows = pl.ds(part * share, share)
        copies.append(pltpu.make_async_copy(update.at[rows], update_hbm.at[rows], sems.at[2 + part]))
        copies[-1].start()
    for copy in copies:
        copy.wait()


def per_device(grads, block_slot, iters_count, stat_left, stat_right):
    smem, vmem, hbm, free = (
        pl.BlockSpec(memory_space=m) for m in (pltpu.SMEM, pltpu.VMEM, pltpu.HBM, pl.ANY)
    )
    dma = pltpu.SemaphoreType.DMA
    stats = jax.ShapeDtypeStruct((CAP, B, B), F32)
    returned, left, right, unit = pl.pallas_call(
        kernel,
        out_shape=(jax.ShapeDtypeStruct((CAP, NDEV, ROWS, B), jnp.int16), stats, stats, jax.ShapeDtypeStruct((8, 128), F32)),
        in_specs=[hbm] * 4,
        out_specs=(free, free, free, vmem),
        scratch_shapes=[pltpu.VMEM((2, NBLK), jnp.int32)]
        + [pltpu.VMEM((NBLK, ROWS, B), BF16)]
        + [pltpu.VMEM((CAP, B, B), F32)] * 4
        + [pltpu.VMEM((CAP, NDEV, ROWS, B), BF16)] * 2
        + [pltpu.VMEM((CAP, NDEV, ROWS, B), jnp.int16)]
        + [pltpu.VMEM((ROWS, 128), F32), pltpu.VMEM((DP, ROWS, 128), F32)]
        + [pltpu.VMEM((ROWS, 128), F32), pltpu.VMEM((MP, ROWS, 128), F32)]
        + [pltpu.VMEM((CAP, NBLK), jnp.int32), pltpu.SMEM((CAP, NBLK), jnp.int32)]
        + [dma((5,)), dma((3, CAP))]
        + [dma((CAP,))] * 6
        + [pltpu.SemaphoreType.REGULAR]
        + [pltpu.VMEM((2, B, B), t) for _, t in PAIRS]
        + [pltpu.VMEM((B, B), t) for _, t in SINGLES],
        compiler_params=pltpu.CompilerParams(
            collective_id=0, has_side_effects=True, vmem_limit_bytes=48 * 2**20
        ),
    )(jnp.stack([block_slot, iters_count]), grads, stat_left, stat_right)
    return pl.pallas_call(
        finish,
        out_shape=(jax.ShapeDtypeStruct((NBLK, ROWS, B), F32), stats, stats),
        in_specs=[smem, vmem, vmem, vmem, vmem],
        out_specs=(hbm, hbm, hbm),
        scratch_shapes=[pltpu.VMEM((NBLK, ROWS, B), F32), dma((4,))],
        compiler_params=pltpu.CompilerParams(vmem_limit_bytes=12 * 2**20),
    )(block_slot, returned, left, right, unit)


def solution(mesh):
    in_specs = (
        P(None, ("dp", "mp"), None),
        P(),
        P(),
        P(("dp", "mp"), None, None),
        P(("dp", "mp"), None, None),
    )
    out_specs = (
        P(None, ("dp", "mp"), None),
        P(("dp", "mp"), None, None),
        P(("dp", "mp"), None, None),
    )
    return jax.shard_map(
        per_device, mesh=mesh, in_specs=in_specs, out_specs=out_specs, check_vma=False
    )
```

```python
import math

import jax
import jax.numpy as jnp
from jax import lax
from jax.experimental import pallas as pl
from jax.experimental.pallas import tpu as pltpu
from jax.sharding import PartitionSpec as P

STAT_DECAY = 0.95
CLIP_SHARE = 0.5
EPSILON = 1e-06

B = 512
NBLK = 128
CAP = 2
NDEV = 128
DP = 8
MP = 16
ROWS = B // NDEV
OCTAVES = 18
LEVELS = 32760.0 / OCTAVES
UNROLL = 127

BF16 = jnp.bfloat16
F32 = jnp.float32
MESH = pl.DeviceIdType.MESH

C5 = [1.25 ** (5 - k) * (-0.25) ** k * math.comb(5, k) for k in range(6)]
V = [1.5625, -0.3125, 0.0, 0.0, 0.0, 0.0, 0.0]
for _k in range(6):
    V[_k + 1] -= C5[_k] / 4


def dot(former, latter):
    return jnp.dot(former, latter, preferred_element_type=F32)


def split(value):
    high = value.astype(BF16)
    return high, (value - high.astype(F32)).astype(BF16)


def total(value):
    return jnp.sum(jnp.sum(value, axis=0, keepdims=True), axis=1, keepdims=True)


def partner(step):
    dp, mp = lax.axis_index("dp"), lax.axis_index("mp")
    offset = (step * 91) & (NDEV - 1)
    core = (dp + offset) & 1
    z = ((dp >> 1) + (offset >> 1)) & 3
    y = ((mp >> 2) + (offset >> 3)) & 3
    x = (mp + (offset >> 5)) & 3
    return z * 2 + core, y * 4 + x


HALF = B // 2
LOW, HIGH, ALL = slice(0, HALF), slice(HALF, B), slice(0, B)
UPPER = ((LOW, ALL), (HIGH, HIGH))


def put(ref, top, corner):
    ref[LOW, :] = top
    ref[HIGH, HIGH] = corner
    ref[HIGH, LOW] = jnp.transpose(top[:, HIGH])


def put_split(high, low, top, corner):
    (top_high, top_low), (corner_high, corner_low) = split(top), split(corner)
    put(high, top_high, corner_high)
    put(low, top_low, corner_low)


def upper(former, latter):
    return dot(former[LOW, :], latter[...]), dot(former[HIGH, :], latter[:, HIGH])


def upper_split(f_high, f_low, l_high, l_low):
    return tuple(
        dot(f_high[rows, :], l_high[:, cols])
        + dot(f_high[rows, :], l_low[:, cols])
        + dot(f_low[rows, :], l_high[:, cols])
        for rows, cols in UPPER
    )


def wide(ref, at):
    return ref[at].astype(F32)


def roots_and_product(g, sl, sr, nl, nr, squared, live, three, s):
    fs = []
    for side, (stat, fresh) in enumerate(((sl, nl), (sr, nr))):
        sums = []
        for rows, cols in UPPER:
            if side == 0:
                former, latter, over = g[rows, :], g[cols, :], 1
            else:
                former, latter, over = g[:, rows], g[:, cols], 0
            gram = lax.dot_general(former, latter, (((over,), (over,)), ((), ())), preferred_element_type=F32)
            targets = [((rows, cols), gram)]
            if rows == LOW:
                targets.append(((HIGH, LOW), jnp.transpose(gram[:, HIGH])))
            for at, part in targets:
                old = stat[at]
                a = jnp.where(live, STAT_DECAY * old + squared * part, old)
                fresh[at] = a
                sums.append(total(a * a))
        fs.append(1.0 / jnp.sqrt(sums[0] + sums[1] + sums[2]))
    a_of = (nl, nr)
    both = (0, 1)
    at2 = lambda name, i: s[name].at[i]
    for i in both:
        s["mh"][i], s["ml"][i] = split(a_of[i][...] * fs[i])
    for i in both:
        square = upper(at2("mh", i), at2("mh", i))
        d = [(a_of[i][at] * (-0.625 * fs[i]) + v * 0.0625).astype(BF16) for at, v in zip(UPPER, square)]
        put(at2("d", i), *d)
    for i in both:
        square = upper(at2("d", i), at2("d", i))
        f = [wide(at2("d", i), at) * 3.125 + v for at, v in zip(UPPER, square)]
        put_split(at2("fh", i), at2("fl", i), *f)
    for i in both:
        product = upper_split(at2("fh", i), at2("fl", i), at2("mh", i), at2("ml", i))
        n = [a_of[i][at] * (1.25**4 * fs[i]) + v for at, v in zip(UPPER, product)]
        for at, v in zip(UPPER, n):
            at2("n", i)[at] = v
        put_split(at2("nh", i), at2("nl", i), *n)
    for i in both:
        square = upper_split(at2("nh", i), at2("nl", i), at2("nh", i), at2("nl", i))
        put(at2("s", i), *[v.astype(BF16) for v in square])
    for i in both:
        c = upper(at2("s", i), at2("nh", i))
        put(at2("c", i), *[v.astype(BF16) for v in c])
        last = [
            V[4] * wide(at2("nh", i), at) + V[5] * wide(at2("s", i), at) + V[6] * v
            for at, v in zip(UPPER, c)
        ]
        put(at2("b", i), *[v.astype(BF16) for v in last])
    w0, w1 = jnp.where(three, V[0], 1.25), jnp.where(three, V[1], -0.25)
    w2, w3, w4 = jnp.where(three, V[2], 0.0), jnp.where(three, V[3], 0.0), jnp.where(three, 1.0, 0.0)
    for i in both:
        product = upper(at2("c", i), at2("b", i))
        u = [
            w1 * at2("n", i)[at] + w2 * wide(at2("s", i), at) + w3 * wide(at2("c", i), at) + w4 * v
            for at, v in zip(UPPER, product)
        ]
        for at, v in zip(UPPER, u):
            at2("n", i)[at] = v
        put(at2("u", i), *[v.astype(BF16) for v in u])
    for i in both:
        product = upper(at2("mh", i), at2("u", i))
        z = [
            1.25 * at2("n", i)[at] - a_of[i][at] * (fs[i] * w0 * 0.25) - 0.25 * v
            for at, v in zip(UPPER, product)
        ]
        put_split(at2("zh", i), at2("zl", i), *z)
    alpha = 1.25 * w0
    h = alpha * g[...].astype(F32) + dot(s["zh"][0], g[...]) + dot(s["zl"][0], g[...])
    s["p"][...] = h
    s["hh"][...], s["hl"][...] = split(h)
    p = (
        alpha * s["p"][...]
        + dot(s["hh"][...], s["zh"][1])
        + dot(s["hh"][...], s["zl"][1])
        + dot(s["hl"][...], s["zh"][1])
    )
    s["p"][...] = p
    return total(p * p)


PAIRS = [
    ("mh", BF16), ("ml", BF16), ("d", BF16), ("fh", BF16), ("fl", BF16), ("n", F32), ("nh", BF16), ("nl", BF16),
    ("s", BF16), ("c", BF16), ("b", BF16), ("u", BF16), ("zh", BF16), ("zl", BF16),
]
SINGLES = [("hh", BF16), ("hl", BF16), ("p", F32), ("g", BF16)]
NAMES = [name for name, _ in PAIRS + SINGLES]


def kernel(
    tables_hbm, grads_hbm, left_hbm, right_hbm, returned, new_left_hbm, new_right_hbm, unit_out,
    tables, grads, left, right, new_left, new_right, fsend, frecv, rsend, psend, precv, gsend, grecv, plan_v, plan,
    local_sem, out_sem, fs_sem, fr_sem, rs_sem, rr_sem, ps_sem, pr_sem, round_sem, *rest,
):
    s = dict(zip(NAMES, rest, strict=True))
    dp, mp = lax.axis_index("dp"), lax.axis_index("mp")
    me = dp * MP + mp

    barrier = pltpu.get_barrier_semaphore()
    for k in range(1, DP):
        pl.semaphore_signal(barrier, inc=1, device_id=((dp + k) & (DP - 1), mp), device_id_type=MESH)
    for k in range(1, MP):
        pl.semaphore_signal(barrier, inc=1, device_id=(dp, (mp + k) & (MP - 1)), device_id_type=MESH)

    names = pltpu.make_async_copy(tables_hbm, tables, local_sem.at[2])
    rows = pltpu.make_async_copy(grads_hbm, grads, local_sem.at[3])
    loads = [
        pltpu.make_async_copy(left_hbm, left, local_sem.at[0]),
        pltpu.make_async_copy(right_hbm, right, local_sem.at[1]),
    ]
    for load in [names, rows, *loads]:
        load.start()
    names.wait()

    lane = lax.broadcasted_iota(jnp.int32, (NBLK, NBLK), 1)
    marks = jnp.transpose(lane * 4 + jnp.broadcast_to(tables[1:2, :] & 3, (NBLK, NBLK)))
    named = jnp.transpose(jnp.broadcast_to(tables[0:1, :], (NBLK, NBLK)))
    for half in range(CAP):
        found = jnp.where(named == lane + half * NBLK, marks, 0)
        plan_v[pl.ds(half, 1), :] = jnp.max(found, axis=0, keepdims=True)
    to_scalars = pltpu.make_async_copy(plan_v, plan, local_sem.at[4])
    to_scalars.start()

    rows.wait()
    widened = grads[...].astype(F32)
    mine = jnp.sum(widened * widened, axis=0)
    psend[...] = mine[:, 0:128] + mine[:, 128:256] + mine[:, 256:384] + mine[:, 384:512]
    precv[dp] = psend[...]

    to_scalars.wait()

    def place(owner, carry):
        for j in range(CAP):
            at = owner * CAP + j
            fsend[j, owner] = grads[jnp.minimum(plan[at >> 7, at & (NBLK - 1)] >> 2, NBLK - 1)]
        return carry

    lax.fori_loop(0, NDEV, place, 0, unroll=8)
    for j in range(CAP):
        frecv[j, me] = fsend[j, me]

    pl.semaphore_wait(barrier, DP + MP - 2)
    for k in range(1, MP):
        pl.semaphore_signal(round_sem, inc=1, device_id=(dp, (mp + k) & (MP - 1)), device_id_type=MESH)
    for k in range(1, DP):
        pltpu.make_async_remote_copy(
            src_ref=psend, dst_ref=precv.at[dp], send_sem=ps_sem.at[0], recv_sem=pr_sem.at[0],
            device_id=((dp + k) & (DP - 1), mp), device_id_type=MESH,
        ).start()
    pl.semaphore_wait(round_sem, MP - 1)

    def exchange(source, target, j, send_sem, recv_sem):
        def step(k, carry):
            to_dp, to_mp = partner(k)
            pltpu.make_async_remote_copy(
                src_ref=source.at[j, to_dp * MP + to_mp],
                dst_ref=target.at[j, me],
                send_sem=send_sem.at[j],
                recv_sem=recv_sem.at[j],
                device_id=(to_dp, to_mp),
                device_id_type=MESH,
            ).start()
            return carry

        lax.fori_loop(1, NDEV, step, 0, unroll=UNROLL)

    def settle(view, sem):
        pltpu.make_async_copy(view, view, sem).wait()

    def others(buffer, j):
        return buffer.at[j, pl.ds(0, NDEV - 1)]

    exchange(fsend, frecv, 0, fs_sem, fr_sem)
    settle(precv.at[pl.ds(0, DP - 1)], pr_sem.at[0])
    gsend[...] = jnp.sum(precv[...], axis=0)
    grecv[mp] = gsend[...]
    for k in range(1, MP):
        pltpu.make_async_remote_copy(
            src_ref=gsend, dst_ref=grecv.at[mp], send_sem=ps_sem.at[1], recv_sem=pr_sem.at[1],
            device_id=(dp, (mp + k) & (MP - 1)), device_id_type=MESH,
        ).start()
    exchange(fsend, frecv, 1, fs_sem, fr_sem)
    for load in loads:
        load.wait()
    settle(grecv.at[pl.ds(0, MP - 1)], pr_sem.at[1])

    def slot(j, carry):
        settle(others(frecv, j), fr_sem.at[j])
        arrived = frecv[j].reshape(B, B)
        s["g"][...] = arrived
        wide = arrived.astype(F32)
        grad_square = total(wide * wide)
        norm = jnp.sqrt(total(jnp.sum(grecv[...], axis=0)))
        clipping = jnp.minimum(1.0, CLIP_SHARE * B * math.sqrt(NBLK) / (norm + EPSILON))
        bound = clipping * norm * (4.0 * norm / (4.0 * norm + EPSILON))
        unit = jnp.maximum(bound * 2.0**-OCTAVES, 1e-30)
        unit_out[...] = jnp.broadcast_to(unit, (8, 128))
        my_slot = me * CAP + j
        granted = plan[my_slot >> 7, my_slot & (NBLK - 1)] & 3
        prod_square = roots_and_product(
            s["g"], left.at[j], right.at[j], new_left.at[j], new_right.at[j],
            clipping * clipping, granted > 0, granted > 2, s,
        )
        pltpu.make_async_copy(new_left.at[j], new_left_hbm.at[j], out_sem.at[0, j]).start()
        pltpu.make_async_copy(new_right.at[j], new_right_hbm.at[j], out_sem.at[1, j]).start()
        graft = clipping * jnp.sqrt(grad_square) / (jnp.sqrt(prod_square) + EPSILON)
        product = s["p"][...]
        level = jnp.round(jnp.log2(1.0 + jnp.abs(product) * (graft / unit)) * LEVELS)
        level = jnp.where(product < 0.0, -level, level).astype(jnp.int32).astype(jnp.int16)
        rsend[j] = level.reshape(NDEV, ROWS, B)
        exchange(rsend, returned, j, rs_sem, rr_sem)
        pltpu.make_async_copy(rsend.at[j, me], returned.at[j, me], out_sem.at[2, j]).start()
        return carry

    lax.fori_loop(0, CAP, slot, 0)

    for j in range(CAP):
        pltpu.make_async_copy(new_left.at[j], new_left_hbm.at[j], out_sem.at[0, j]).wait()
        pltpu.make_async_copy(new_right.at[j], new_right_hbm.at[j], out_sem.at[1, j]).wait()
        pltpu.make_async_copy(rsend.at[j, me], returned.at[j, me], out_sem.at[2, j]).wait()
        settle(others(fsend, j), fs_sem.at[j])
        settle(others(rsend, j), rs_sem.at[j])
    settle(precv.at[pl.ds(0, DP - 1)], ps_sem.at[0])
    settle(grecv.at[pl.ds(0, MP - 1)], ps_sem.at[1])
    for j in range(CAP):
        settle(others(returned, j), rr_sem.at[j])


def finish(slot_of, returned, left, right, unit, update_hbm, new_left_hbm, new_right_hbm, update, sems):
    copies = [
        pltpu.make_async_copy(left, new_left_hbm, sems.at[0]),
        pltpu.make_async_copy(right, new_right_hbm, sems.at[1]),
    ]
    for copy in copies:
        copy.start()

    def gather(b, carry):
        at = slot_of[b]
        piece = returned[at & 1, at >> 1]
        level = piece.astype(jnp.int32).astype(F32)
        size = (jnp.exp2(jnp.abs(level) * (1.0 / LEVELS)) - 1.0) * unit[0:1, 0:1]
        update[b] = jnp.where(level < 0.0, -size, size)
        return carry

    share = NBLK // 2
    for part in range(2):
        lax.fori_loop(part * share, (part + 1) * share, gather, 0, unroll=8)
        rows = pl.ds(part * share, share)
        copies.append(pltpu.make_async_copy(update.at[rows], update_hbm.at[rows], sems.at[2 + part]))
        copies[-1].start()
    for copy in copies:
        copy.wait()


def per_device(grads, block_slot, iters_count, stat_left, stat_right):
    smem, vmem, hbm, free = (
        pl.BlockSpec(memory_space=m) for m in (pltpu.SMEM, pltpu.VMEM, pltpu.HBM, pl.ANY)
    )
    dma = pltpu.SemaphoreType.DMA
    stats = jax.ShapeDtypeStruct((CAP, B, B), F32)
    returned, left, right, unit = pl.pallas_call(
        kernel,
        out_shape=(jax.ShapeDtypeStruct((CAP, NDEV, ROWS, B), jnp.int16), stats, stats, jax.ShapeDtypeStruct((8, 128), F32)),
        in_specs=[hbm] * 4,
        out_specs=(free, free, free, vmem),
        scratch_shapes=[pltpu.VMEM((2, NBLK), jnp.int32)]
        + [pltpu.VMEM((NBLK, ROWS, B), BF16)]
        + [pltpu.VMEM((CAP, B, B), F32)] * 4
        + [pltpu.VMEM((CAP, NDEV, ROWS, B), BF16)] * 2
        + [pltpu.VMEM((CAP, NDEV, ROWS, B), jnp.int16)]
        + [pltpu.VMEM((ROWS, 128), F32), pltpu.VMEM((DP, ROWS, 128), F32)]
        + [pltpu.VMEM((ROWS, 128), F32), pltpu.VMEM((MP, ROWS, 128), F32)]
        + [pltpu.VMEM((CAP, NBLK), jnp.int32), pltpu.SMEM((CAP, NBLK), jnp.int32)]
        + [dma((5,)), dma((3, CAP))]
        + [dma((CAP,))] * 6
        + [pltpu.SemaphoreType.REGULAR]
        + [pltpu.VMEM((2, B, B), t) for _, t in PAIRS]
        + [pltpu.VMEM((B, B), t) for _, t in SINGLES],
        compiler_params=pltpu.CompilerParams(
            collective_id=0, has_side_effects=True, vmem_limit_bytes=48 * 2**20
        ),
    )(jnp.stack([block_slot, iters_count]), grads, stat_left, stat_right)
    return pl.pallas_call(
        finish,
        out_shape=(jax.ShapeDtypeStruct((NBLK, ROWS, B), F32), stats, stats),
        in_specs=[smem, vmem, vmem, vmem, vmem],
        out_specs=(hbm, hbm, hbm),
        scratch_shapes=[pltpu.VMEM((NBLK, ROWS, B), F32), dma((4,))],
        compiler_params=pltpu.CompilerParams(vmem_limit_bytes=12 * 2**20),
    )(block_slot, returned, left, right, unit)


def solution(mesh):
    in_specs = (
        P(None, ("dp", "mp"), None),
        P(),
        P(),
        P(("dp", "mp"), None, None),
        P(("dp", "mp"), None, None),
    )
    out_specs = (
        P(None, ("dp", "mp"), None),
        P(("dp", "mp"), None, None),
        P(("dp", "mp"), None, None),
    )
    return jax.shard_map(
        per_device, mesh=mesh, in_specs=in_specs, out_specs=out_specs, check_vma=False
    )
```
